256 devices in a mesh: scen: 2 (over core), tx: 8 (over y, x_lo), ty: 16 (over x_hi, z).
Axes of the slice: x: 4 (x_hi: 2, x_lo: 2; x = x_hi * 2 + x_lo), y: 4, z: 8, core: 2. Of those that a mesh axis runs over, the one named last changes fastest.
Arguments:
- conductivity: float32 [512, 512, 128], P('tx', 'ty'), may hold values from 0.1 to 1
- cooling: float32 [2, 512, 512, 128], P('scen', 'tx', 'ty'), may hold values from 0.2 to 1.5
- source: float32 [2, 512, 512, 128], P('scen', 'tx', 'ty'), may hold values from -6 to 6
- adjoint_in: float32 [2, 512, 512, 128], P('scen', 'tx', 'ty'), may hold values from -6 to 6
- store: float32 [2, 6, 128, 128, 2048], P('scen', None, ('tx', 'ty')), may hold values from -6 to 6
- holder: int32 [128, 128], P(('tx', 'ty')), may hold values from 0 to 127, each once within a row
- step_index: int32 [2], P('scen'), may hold values from 0 to 5
Outputs:
- adjoint_out: float32 [2, 512, 512, 128], P('scen', 'tx', 'ty')
- grad_conductivity: float32 [512, 512, 128], P('tx', 'ty')
The draws below stay inside these ranges and needn't reach their ends.
Inputs may be any that keep to these rules, and one draw needn't show every extreme that they name: Each row of holder names each of the 128 devices of tx+ty exactly once.
All inputs are finite; a program needn't handle non-finite values.
Results may differ from the reference program's by a relative error of at most 0.00002.
Values sent between devices are 32-bit elements; how exact they have to be, the bound alone decides.
A program may use at most 64 MiB of HBM per device.

```python
import math
import jax
import jax.numpy as jnp
from jax import lax

CX = 64
CY = 32
NZ = 128
NCK = 6
S = 2
TILES = 128
PIECE = 2048
NX = 512
NY = 512
N_TX = 8
N_TY = 16


def levels(key, extent, shards, low, high):
    def one(position, blocks):
        heights = jax.random.uniform(jax.random.fold_in(jax.random.fold_in(key, 6), position), (blocks,), jnp.float32, low / len(shards), high / len(shards))
        return jnp.repeat(jnp.exp(heights), extent[position] // blocks).reshape((-1,) + (1,) * (len(extent) - position - 1))

    level = one(*shards[0])
    for cut in shards[1:]:
        level = level * one(*cut)
    return level


def centred(own_key, dims, scale, limit, split=(), kind=jnp.bfloat16):
    factor_of = levels(own_key, dims, split, -0.22, 0.18) if split else 1.0
    array = jax.random.normal(own_key, dims, jnp.float32) * scale * factor_of
    return jnp.minimum(jnp.maximum(array, -limit), limit).astype(kind)


def setup_inputs(seed: int = 0) -> dict:
    keys = jax.random.split(jax.random.key(seed), 8)
    conductivity = jnp.clip(jnp.exp(math.log(1.0) - 2.3025851 * jax.random.uniform(keys[0], (NX, NY, NZ), jnp.float32) ** levels(keys[0], (NX, NY, NZ), ((0, 8), (1, 16)), -0.2, 0.2)), 0.1, 1.0)
    cooling = jnp.clip(jnp.exp(math.log(1.5) - 2.014903 * jax.random.uniform(keys[1], (S, NX, NY, NZ), jnp.float32) ** levels(keys[1], (S, NX, NY, NZ), ((0, 2), (1, 8), (2, 16)), -0.2, 0.2)), 0.2, 1.5)
    source = centred(keys[2], (S, NX, NY, NZ), 1.0, 6.0, ((0, 2), (1, 8), (2, 16)), jnp.float32)
    adjoint_in = centred(keys[3], (S, NX, NY, NZ), 1.0, 6.0, ((0, 2), (1, 8), (2, 16)), jnp.float32)
    store = centred(keys[4], (S, NCK, TILES, TILES, PIECE), 1.0, 6.0, ((0, 2), (2, 128)), jnp.float32)
    holder = jax.vmap(lambda own: jax.random.permutation(own, TILES))(jax.random.split(keys[5], TILES)).reshape((TILES, TILES)).astype(jnp.int32)
    step_index = jax.random.randint(keys[6], (S,), 0, NCK).astype(jnp.int32)
    return dict(conductivity=conductivity, cooling=cooling, source=source, adjoint_in=adjoint_in, store=store, holder=holder, step_index=step_index)


step_size = 0.12

def flux_total(field, conduct):
    padded = jnp.pad(field, ((1, 1), (1, 1), (0, 0)))
    cond_pad = jnp.pad(conduct, ((1, 1), (1, 1), (0, 0)))
    face_x = (cond_pad[1:, 1:-1] + cond_pad[:-1, 1:-1]) * 0.5 * (padded[1:, 1:-1] - padded[:-1, 1:-1])
    total = face_x[1:] - face_x[:-1]
    face_y = (cond_pad[1:-1, 1:] + cond_pad[1:-1, :-1]) * 0.5 * (padded[1:-1, 1:] - padded[1:-1, :-1])
    total = total + face_y[:, 1:] - face_y[:, :-1]
    face_z = (conduct[:, :, 1:] + conduct[:, :, :-1]) * 0.5 * (field[:, :, 1:] - field[:, :, :-1])
    zero_pad = ((0, 0), (0, 0), (0, 1))
    left_pad = ((0, 0), (0, 0), (1, 0))
    return total + jnp.pad(face_z, zero_pad) - jnp.pad(face_z, left_pad)

def reference(conductivity, cooling, source, adjoint_in, store, holder, step_index):
    scen_ids = jnp.arange(S, dtype=jnp.int32)
    chosen = store[scen_ids, step_index.astype(jnp.int32)]
    tile_ids = jnp.arange(TILES, dtype=jnp.int32)[:, None]
    pieces = chosen[:, holder, tile_ids]
    state_zero = pieces.reshape(S, N_TX, N_TY, CX, CY, NZ).transpose(0, 1, 3, 2, 4, 5).reshape(S, NX, NY, NZ)

    def one_scenario(items):
        start, cool_here, heat_here, adjoint_late = items

        def forward(field, conduct):
            middle_state = field + step_size * (flux_total(field, conduct) - cool_here * field + heat_here)
            return middle_state + step_size * (flux_total(middle_state, conduct) - cool_here * middle_state + heat_here)
        _, pullback = jax.vjp(forward, start, conductivity)
        return pullback(adjoint_late)
    adjoint_out, gradients = lax.map(one_scenario, (state_zero, cooling, source, adjoint_in))
    return (adjoint_out, lax.optimization_barrier(jnp.sum(gradients, axis=0)))
```

```python
import functools

import jax
import jax.numpy as jnp
from jax import lax
from jax.experimental import pallas as pl
from jax.experimental.pallas import tpu as pltpu
from jax.sharding import PartitionSpec as P

MESH = pl.DeviceIdType.MESH
step_size = 0.12


def exchange_kernel(n_ty, tiles, src, dst, send_sem, recv_sem, local_sem):
    scen = lax.axis_index("scen")
    me = lax.axis_index("tx") * n_ty + lax.axis_index("ty")

    def device(k):
        t = (me + k) % tiles
        return t, (scen, t // n_ty, t % n_ty)

    barrier = pltpu.get_barrier_semaphore()

    def greet(k, carry):
        pl.semaphore_signal(barrier, inc=1, device_id=device(k)[1], device_id_type=MESH)
        return carry

    lax.fori_loop(1, tiles, greet, 0)
    pl.semaphore_wait(barrier, tiles - 1)
    own = pltpu.make_async_copy(src.at[me], dst.at[me], local_sem)
    own.start()

    def send(k, carry):
        t, target = device(k)
        pltpu.make_async_remote_copy(
            src_ref=src.at[t],
            dst_ref=dst.at[me],
            send_sem=send_sem,
            recv_sem=recv_sem,
            device_id=target,
            device_id_type=MESH,
        ).start()
        return carry

    lax.fori_loop(1, tiles, send, 0)
    own.wait()
    others = pl.ds(0, tiles - 1)
    pltpu.make_async_copy(src.at[others], src.at[others], send_sem).wait()
    pltpu.make_async_copy(dst.at[others], dst.at[others], recv_sem).wait()


def exchange(pieces, n_ty):
    tiles = pieces.shape[0]
    return pl.pallas_call(
        functools.partial(exchange_kernel, n_ty, tiles),
        out_shape=jax.ShapeDtypeStruct(pieces.shape, pieces.dtype),
        in_specs=[pl.BlockSpec(memory_space=pltpu.VMEM)],
        out_specs=pl.BlockSpec(memory_space=pltpu.VMEM),
        scratch_shapes=[pltpu.SemaphoreType.DMA] * 3,
        compiler_params=pltpu.CompilerParams(collective_id=0, has_side_effects=True),
    )(pieces)


def assemble_kernel(holder, arrived, state):
    def place(j, carry):
        state[j] = arrived[holder[j]]
        return carry

    lax.fori_loop(0, state.shape[0], place, 0, unroll=8)


def assemble(arrived, holder):
    return pl.pallas_call(
        assemble_kernel,
        out_shape=jax.ShapeDtypeStruct(arrived.shape, arrived.dtype),
        in_specs=[pl.BlockSpec(memory_space=pltpu.SMEM), pl.BlockSpec(memory_space=pltpu.VMEM)],
        out_specs=pl.BlockSpec(memory_space=pltpu.VMEM),
    )(holder, arrived)


def padded_2(block, sides, width):
    for axis, dim in sides:
        count = lax.axis_size(axis)
        forward = [(i, i + 1) for i in range(count - 1)]
        backward = [(target, source) for source, target in forward]
        low = lax.ppermute(
            lax.slice_in_dim(block, block.shape[dim] - width, None, axis=dim), axis, forward
        )
        high = lax.ppermute(lax.slice_in_dim(block, 0, width, axis=dim), axis, backward)
        block = jnp.concatenate([low, block, high], axis=dim)
    return block


def flux_total(padded, cond_pad):
    face_x = (
        (cond_pad[1:, 1:-1] + cond_pad[:-1, 1:-1]) * 0.5 * (padded[1:, 1:-1] - padded[:-1, 1:-1])
    )
    total = face_x[1:] - face_x[:-1]
    face_y = (
        (cond_pad[1:-1, 1:] + cond_pad[1:-1, :-1]) * 0.5 * (padded[1:-1, 1:] - padded[1:-1, :-1])
    )
    total = total + face_y[:, 1:] - face_y[:, :-1]
    inner_field = padded[1:-1, 1:-1]
    inner_cond = cond_pad[1:-1, 1:-1]
    face_z = (
        (inner_cond[:, :, 1:] + inner_cond[:, :, :-1])
        * 0.5
        * (inner_field[:, :, 1:] - inner_field[:, :, :-1])
    )
    zero_pad = ((0, 0), (0, 0), (0, 1))
    left_pad = ((0, 0), (0, 0), (1, 0))
    return total + jnp.pad(face_z, zero_pad) - jnp.pad(face_z, left_pad)


def face_products(state_pad, adjoint_pad):
    prod_x = (state_pad[1:, 1:-1] - state_pad[:-1, 1:-1]) * (
        adjoint_pad[1:, 1:-1] - adjoint_pad[:-1, 1:-1]
    )
    total = prod_x[1:] + prod_x[:-1]
    prod_y = (state_pad[1:-1, 1:] - state_pad[1:-1, :-1]) * (
        adjoint_pad[1:-1, 1:] - adjoint_pad[1:-1, :-1]
    )
    total = total + prod_y[:, 1:] + prod_y[:, :-1]
    inner_state = state_pad[1:-1, 1:-1]
    inner_adjoint = adjoint_pad[1:-1, 1:-1]
    prod_z = (inner_state[:, :, 1:] - inner_state[:, :, :-1]) * (
        inner_adjoint[:, :, 1:] - inner_adjoint[:, :, :-1]
    )
    zero_pad = ((0, 0), (0, 0), (0, 1))
    left_pad = ((0, 0), (0, 0), (1, 0))
    total = total + jnp.pad(prod_z, zero_pad) + jnp.pad(prod_z, left_pad)
    return -0.5 * step_size * total


def state_halo(field):
    return padded_2(field, (("tx", 0), ("ty", 1)), 1)


def local(conductivity, cooling, source, adjoint_in, store, holder, step_index):
    cells_x, cells_y, cells_z = conductivity.shape
    chosen = lax.dynamic_index_in_dim(store[0, :, 0], step_index[0], 0, keepdims=False)
    arrived = exchange(chosen.reshape(chosen.shape[0], -1, cells_z), lax.axis_size("ty"))
    state_zero = assemble(arrived, holder[0]).reshape(cells_x, cells_y, cells_z)
    cool_here = cooling[0]
    heat_here = source[0]
    adjoint_late = adjoint_in[0]
    near_coeffs = padded_2(jnp.stack([conductivity, adjoint_late]), (("tx", 1), ("ty", 2)), 1)
    cond_near = near_coeffs[0]
    late_near = near_coeffs[1]
    state_near = state_halo(state_zero)
    second_state = state_zero + step_size * (
        flux_total(state_near, cond_near) - cool_here * state_zero + heat_here
    )
    second_near = state_halo(second_state)
    middle_adjoint = adjoint_late + step_size * (
        flux_total(late_near, cond_near) - cool_here * adjoint_late
    )
    middle_near = state_halo(middle_adjoint)
    middle_inner = middle_near[1:-1, 1:-1]
    gradient = face_products(second_near, late_near) + face_products(state_near, middle_near)
    earliest = middle_inner + step_size * (
        flux_total(middle_near, cond_near) - cool_here * middle_inner
    )
    summed = gradient + lax.ppermute(gradient, "scen", [(0, 1), (1, 0)])
    return (earliest[None], summed)


def solution(mesh):
    in_specs = (
        P("tx", "ty", None),
        P("scen", "tx", "ty", None),
        P("scen", "tx", "ty", None),
        P("scen", "tx", "ty", None),
        P("scen", None, ("tx", "ty"), None, None),
        P(("tx", "ty"), None),
        P("scen"),
    )
    out_specs = (P("scen", "tx", "ty", None), P("tx", "ty", None))
    return jax.shard_map(local, mesh=mesh, in_specs=in_specs, out_specs=out_specs, check_vma=False)
```

```python
import functools

import jax
import jax.numpy as jnp
from jax import lax
from jax.experimental import pallas as pl
from jax.experimental.pallas import tpu as pltpu
from jax.sharding import PartitionSpec as P

MESH = pl.DeviceIdType.MESH
step_size = 0.12


def exchange_kernel(n_ty, tiles, rows, step, store, dst, saved, src, send_sem, recv_sem, local_sem, load_sem):
    scen = lax.axis_index("scen")
    me = lax.axis_index("tx") * n_ty + lax.axis_index("ty")
    lanes = src.shape[1]
    load = pltpu.make_async_copy(store, saved, load_sem)
    load.start()

    def device(k):
        t = (me + k) % tiles
        return t, (scen, t // n_ty, t % n_ty)

    def piece(t):
        return pl.ds(pl.multiple_of(t * rows, rows), rows)

    barrier = pltpu.get_barrier_semaphore()

    def greet(k, carry):
        pl.semaphore_signal(barrier, inc=1, device_id=device(k)[1], device_id_type=MESH)
        return carry

    lax.fori_loop(1, tiles, greet, 0)
    load.wait()
    chosen = step[0]

    def unfold(g, carry):
        for r in range(rows):
            src[pl.ds(g * 8 * rows + r, 8, stride=rows), :] = saved[
                chosen, pl.ds(pl.multiple_of(g * 8, 8), 8), pl.ds(r * lanes, lanes)
            ]
        return carry

    lax.fori_loop(0, tiles // 8, unfold, 0)
    pl.semaphore_wait(barrier, tiles - 1)
    own = pltpu.make_async_copy(src.at[piece(me)], dst.at[piece(me)], local_sem)
    own.start()

    def send(k, carry):
        t, target = device(k)
        pltpu.make_async_remote_copy(
            src_ref=src.at[piece(t)],
            dst_ref=dst.at[piece(me)],
            send_sem=send_sem,
            recv_sem=recv_sem,
            device_id=target,
            device_id_type=MESH,
        ).start()
        return carry

    lax.fori_loop(1, tiles, send, 0)
    own.wait()
    others = pl.ds(0, (tiles - 1) * rows)
    pltpu.make_async_copy(src.at[others], src.at[others], send_sem).wait()
    pltpu.make_async_copy(dst.at[others], dst.at[others], recv_sem).wait()


def exchange(store, step_index, n_ty, lanes):
    tiles, piece = store.shape[1:]
    rows = piece // lanes
    flat = (tiles * rows, lanes)
    arrived = pl.pallas_call(
        functools.partial(exchange_kernel, n_ty, tiles, rows),
        out_shape=jax.ShapeDtypeStruct(flat, store.dtype),
        in_specs=[
            pl.BlockSpec(memory_space=pltpu.SMEM),
            pl.BlockSpec(memory_space=pltpu.HBM),
        ],
        out_specs=pl.BlockSpec(memory_space=pltpu.VMEM),
        scratch_shapes=[
            pltpu.VMEM(store.shape, store.dtype),
            pltpu.VMEM(flat, store.dtype),
            *[pltpu.SemaphoreType.DMA] * 4,
        ],
        compiler_params=pltpu.CompilerParams(
            collective_id=0, has_side_effects=True, vmem_limit_bytes=32 << 20
        ),
    )(step_index, store)
    return arrived.reshape(tiles, rows, lanes)


def assemble_kernel(holder, arrived, state):
    def place(j, carry):
        state[j] = arrived[holder[j]]
        return carry

    lax.fori_loop(0, state.shape[0], place, 0, unroll=8)


def assemble(arrived, holder):
    return pl.pallas_call(
        assemble_kernel,
        out_shape=jax.ShapeDtypeStruct(arrived.shape, arrived.dtype),
        in_specs=[pl.BlockSpec(memory_space=pltpu.SMEM), pl.BlockSpec(memory_space=pltpu.VMEM)],
        out_specs=pl.BlockSpec(memory_space=pltpu.VMEM),
    )(holder, arrived)


def padded_2(block, sides, width):
    for axis, dim in sides:
        count = lax.axis_size(axis)
        forward = [(i, i + 1) for i in range(count - 1)]
        backward = [(target, source) for source, target in forward]
        low = lax.ppermute(
            lax.slice_in_dim(block, block.shape[dim] - width, None, axis=dim), axis, forward
        )
        high = lax.ppermute(lax.slice_in_dim(block, 0, width, axis=dim), axis, backward)
        block = jnp.concatenate([low, block, high], axis=dim)
    return block


def flux_total(padded, cond_pad):
    face_x = (
        (cond_pad[1:, 1:-1] + cond_pad[:-1, 1:-1]) * 0.5 * (padded[1:, 1:-1] - padded[:-1, 1:-1])
    )
    total = face_x[1:] - face_x[:-1]
    face_y = (
        (cond_pad[1:-1, 1:] + cond_pad[1:-1, :-1]) * 0.5 * (padded[1:-1, 1:] - padded[1:-1, :-1])
    )
    total = total + face_y[:, 1:] - face_y[:, :-1]
    inner_field = padded[1:-1, 1:-1]
    inner_cond = cond_pad[1:-1, 1:-1]
    face_z = (
        (inner_cond[:, :, 1:] + inner_cond[:, :, :-1])
        * 0.5
        * (inner_field[:, :, 1:] - inner_field[:, :, :-1])
    )
    zero_pad = ((0, 0), (0, 0), (0, 1))
    left_pad = ((0, 0), (0, 0), (1, 0))
    return total + jnp.pad(face_z, zero_pad) - jnp.pad(face_z, left_pad)


def face_products(state_pad, adjoint_pad):
    prod_x = (state_pad[1:, 1:-1] - state_pad[:-1, 1:-1]) * (
        adjoint_pad[1:, 1:-1] - adjoint_pad[:-1, 1:-1]
    )
    total = prod_x[1:] + prod_x[:-1]
    prod_y = (state_pad[1:-1, 1:] - state_pad[1:-1, :-1]) * (
        adjoint_pad[1:-1, 1:] - adjoint_pad[1:-1, :-1]
    )
    total = total + prod_y[:, 1:] + prod_y[:, :-1]
    inner_state = state_pad[1:-1, 1:-1]
    inner_adjoint = adjoint_pad[1:-1, 1:-1]
    prod_z = (inner_state[:, :, 1:] - inner_state[:, :, :-1]) * (
        inner_adjoint[:, :, 1:] - inner_adjoint[:, :, :-1]
    )
    zero_pad = ((0, 0), (0, 0), (0, 1))
    left_pad = ((0, 0), (0, 0), (1, 0))
    total = total + jnp.pad(prod_z, zero_pad) + jnp.pad(prod_z, left_pad)
    return -0.5 * step_size * total


def state_halo(field):
    return padded_2(field, (("tx", 0), ("ty", 1)), 1)


def local(conductivity, cooling, source, adjoint_in, store, holder, step_index):
    cells_x, cells_y, cells_z = conductivity.shape
    arrived = exchange(store[0, :, 0], step_index, lax.axis_size("ty"), cells_z)
    state_zero = assemble(arrived, holder[0]).reshape(cells_x, cells_y, cells_z)
    cool_here = cooling[0]
    heat_here = source[0]
    adjoint_late = adjoint_in[0]
    near_coeffs = padded_2(jnp.stack([conductivity, adjoint_late]), (("tx", 1), ("ty", 2)), 1)
    cond_near = near_coeffs[0]
    late_near = near_coeffs[1]
    state_near = state_halo(state_zero)
    second_state = state_zero + step_size * (
        flux_total(state_near, cond_near) - cool_here * state_zero + heat_here
    )
    second_near = state_halo(second_state)
    middle_adjoint = adjoint_late + step_size * (
        flux_total(late_near, cond_near) - cool_here * adjoint_late
    )
    middle_near = state_halo(middle_adjoint)
    middle_inner = middle_near[1:-1, 1:-1]
    gradient = face_products(second_near, late_near) + face_products(state_near, middle_near)
    earliest = middle_inner + step_size * (
        flux_total(middle_near, cond_near) - cool_here * middle_inner
    )
    summed = gradient + lax.ppermute(gradient, "scen", [(0, 1), (1, 0)])
    return (earliest[None], summed)


def solution(mesh):
    in_specs = (
        P("tx", "ty", None),
        P("scen", "tx", "ty", None),
        P("scen", "tx", "ty", None),
        P("scen", "tx", "ty", None),
        P("scen", None, ("tx", "ty"), None, None),
        P(("tx", "ty"), None),
        P("scen"),
    )
    out_specs = (P("scen", "tx", "ty", None), P("tx", "ty", None))
    return jax.shard_map(local, mesh=mesh, in_specs=in_specs, out_specs=out_specs, check_vma=False)
```

```python
import functools

import jax
import jax.numpy as jnp
from jax import lax
from jax.experimental import pallas as pl
from jax.experimental.pallas import tpu as pltpu
from jax.sharding import PartitionSpec as P

MESH = pl.DeviceIdType.MESH
step_size = 0.12
TOP = 8
COND, LATE, MIDDLE, START, SECOND = range(5)
X_LOW, X_HIGH, Y_LOW, Y_HIGH = range(4)
CHUNKS = 4
UNROLL = 8


def window_kernel(
    sizes,
    step, holder, cond_in, cool_in, heat_in, late_in, store,
    earliest, mine, theirs, edge_mine, edge_theirs,
    saved, outbox, inbox, cond_raw, late_raw, decay, heat,
    cond, late, middle, start, second,
    cond_x, cond_y, cond_z, late_x, late_y, late_z, middle_x, middle_y, middle_z,
    halo_x, halo_y, pack_y,
    load_sem, own_sem, piece_send, piece_recv, halo_send, halo_recv, core_send, core_recv,
):
    n_tx, n_ty, cells_x, cells_y, cells_z, tiles, rows = sizes
    scen, tx, ty = lax.axis_index("scen"), lax.axis_index("tx"), lax.axis_index("ty")
    me = tx * n_ty + ty
    f32 = jnp.float32

    loads = [
        pltpu.make_async_copy(source, target, load_sem.at[i])
        for i, (source, target) in enumerate(
            [(store, saved), (cond_in, cond_raw), (late_in, late_raw), (cool_in, decay), (heat_in, heat)]
        )
    ]
    for load in loads:
        load.start()

    def device(k):
        t = (me + k) % tiles
        return t, (scen, t // n_ty, t % n_ty)

    other_core = (1 - scen, tx, ty)
    barrier = pltpu.get_barrier_semaphore()

    def greet(k, carry):
        pl.semaphore_signal(barrier, inc=1, device_id=device(k)[1], device_id_type=MESH)
        return carry

    lax.fori_loop(1, tiles, greet, 0)
    pl.semaphore_signal(barrier, inc=1, device_id=other_core, device_id_type=MESH)

    def plane(x):
        return pl.ds(pl.multiple_of(x * cells_y, cells_y), cells_y)

    def piece(t):
        return pl.ds(pl.multiple_of(t * rows, rows), rows)

    here, above, below = pl.ds(TOP, cells_y), pl.ds(TOP + 1, cells_y), pl.ds(TOP - 1, cells_y)
    depth = cond.shape[1]

    def edge_rows(ref, y, first=1):
        flat = ref.reshape(ref.shape[0] * depth, cells_z)
        return flat, pl.ds(first * depth + TOP + y, cells_x, stride=depth)

    there = [tx > 0, tx < n_tx - 1, ty > 0, ty < n_ty - 1]
    neighbour = [(scen, tx - 1, ty), (scen, tx + 1, ty), (scen, tx, ty - 1), (scen, tx, ty + 1)]

    def x_slot(field, side):
        return pl.ds((field * 2 + side) * cells_y, cells_y)

    def y_slot(field, side):
        return pl.ds((field * 2 + side) * cells_x, cells_x)

    def landing(field, side):
        if side < 2:
            return halo_x.at[x_slot(field, side)]
        return halo_y.at[y_slot(field, side - 2)]

    def edge_copy(field, ref, side):
        if side < 2:
            source = ref.at[1 if side == X_LOW else cells_x, here]
        else:
            source = pack_y.at[y_slot(field, side - 2)]
        return pltpu.make_async_remote_copy(
            src_ref=source,
            dst_ref=landing(field, side ^ 1),
            send_sem=halo_send.at[field * 4 + side],
            recv_sem=halo_recv.at[field * 4 + (side ^ 1)],
            device_id=neighbour[side],
            device_id_type=MESH,
        )

    def pack(field, ref):
        for side, y in ((0, 0), (1, cells_y - 1)):
            flat, where = edge_rows(ref, y)
            pack_y[y_slot(field, side), :] = flat[where, :]

    def send_edges(field, ref):
        for side in range(4):
            @pl.when(there[side])
            def _():
                edge_copy(field, ref, side).start()

    def wait_edges(field):
        for side in range(4):
            @pl.when(there[side])
            def _():
                slot = landing(field, side)
                pltpu.make_async_copy(slot, slot, halo_recv.at[field * 4 + side]).wait()

    def unpack(field, ref):
        for side, y in ((0, -1), (1, cells_y)):
            ref[0 if side == 0 else cells_x + 1, here] = halo_x[x_slot(field, side), :]
            flat, where = edge_rows(ref, y)
            flat[where, :] = halo_y[y_slot(field, side), :]

    for side in range(4):
        @pl.when(jnp.logical_not(there[side]))
        def _():
            for field in range(5):
                slot = landing(field, side)
                slot[...] = jnp.zeros(slot.shape, f32)

    def clear(i, carry):
        for ref in (start, second):
            ref[i, pl.ds(0, TOP)] = jnp.zeros((TOP, cells_z), f32)
            ref[i, pl.ds(TOP + cells_y, TOP)] = jnp.zeros((TOP, cells_z), f32)
        return carry

    lax.fori_loop(1, cells_x + 1, clear, 0, unroll=UNROLL)
    for ref in (start, second):
        for i in (0, cells_x + 1):
            ref[i, here] = jnp.zeros((cells_y, cells_z), f32)

    loads[1].wait()
    loads[2].wait()

    def lay(x, carry):
        cond[x + 1, here] = cond_raw[plane(x), :] * (0.5 * step_size)
        late[x + 1, here] = late_raw[plane(x), :]
        return carry

    lax.fori_loop(0, cells_x, lay, 0, unroll=UNROLL)
    pack(COND, cond)
    pack(LATE, late)

    loads[0].wait()
    chosen = step[0]

    def unfold(g, carry):
        for r in range(rows):
            outbox[pl.ds(g * 8 * rows + r, 8, stride=rows), :] = saved[
                chosen, pl.ds(pl.multiple_of(g * 8, 8), 8), pl.ds(r * cells_z, cells_z)
            ]
        return carry

    lax.fori_loop(0, tiles // 8, unfold, 0)
    loads[3].wait()
    loads[4].wait()

    def scale(x, carry):
        decay[plane(x), :] = 1.0 - step_size * decay[plane(x), :]
        heat[plane(x), :] = step_size * heat[plane(x), :]
        return carry

    lax.fori_loop(0, cells_x, scale, 0, unroll=UNROLL)

    pl.semaphore_wait(barrier, tiles)

    send_edges(COND, cond)
    send_edges(LATE, late)

    def send(k, carry):
        t, target = device(k)
        pltpu.make_async_remote_copy(
            src_ref=outbox.at[piece(t)],
            dst_ref=inbox.at[me],
            send_sem=piece_send,
            recv_sem=piece_recv,
            device_id=target,
            device_id_type=MESH,
        ).start()
        return carry

    half = tiles // 2
    lax.fori_loop(1, half, send, 0)
    own = pltpu.make_async_copy(outbox.at[piece(me)], inbox.at[me], own_sem)
    own.start()

    lane = lax.broadcasted_iota(jnp.int32, (cells_y, cells_z), 1)
    inner = jnp.where(lane < cells_z - 1, f32(1), f32(0))
    slope = -0.5 * step_size

    def next_z(value):
        return pltpu.roll(value, cells_z - 1, 1)

    def last_z(value):
        return pltpu.roll(value, 1, 1)

    wait_edges(COND)
    wait_edges(LATE)
    unpack(COND, cond)
    unpack(LATE, late)

    def first_face(ref):
        return ref[1, here] - ref[0, here]

    kx = cond[0, here] + cond[1, here]
    dx = first_face(late)
    cond_x[plane(0), :] = kx
    late_x[plane(0), :] = slope * dx

    def middle_plane(i, carry):
        k, w, flux = carry
        k_next, w_next = cond[i + 1, here], late[i + 1, here]
        kx, dx = k + k_next, w_next - w
        cond_x[plane(i), :] = kx
        late_x[plane(i), :] = slope * dx
        flux_next = kx * dx
        ky_up, ky_down = k + cond[i, above], k + cond[i, below]
        d_up, d_down = late[i, above] - w, w - late[i, below]
        cond_y[i, below] = ky_down
        cond_y[i, here] = ky_up
        late_y[i, below] = slope * d_down
        late_y[i, here] = slope * d_up
        kz, dz = (k + next_z(k)) * inner, next_z(w) - w
        cond_z[plane(i - 1), :] = kz
        late_z[plane(i - 1), :] = dz * (slope * inner)
        fz = kz * dz
        middle[i, here] = (
            decay[plane(i - 1), :] * w
            + (flux_next - flux)
            + (ky_up * d_up - ky_down * d_down)
            + (fz - last_z(fz))
        )
        return k_next, w_next, flux_next

    lax.fori_loop(1, cells_x + 1, middle_plane, (cond[1, here], late[1, here], kx * dx), unroll=UNROLL)
    pack(MIDDLE, middle)
    send_edges(MIDDLE, middle)

    lax.fori_loop(half, tiles, send, 0)

    wait_edges(MIDDLE)
    unpack(MIDDLE, middle)
    dx = first_face(middle)
    middle_x[plane(0), :] = slope * dx

    def earliest_plane(i, carry):
        w, flux = carry
        w_next = middle[i + 1, here]
        dx = w_next - w
        middle_x[plane(i), :] = slope * dx
        flux_next = cond_x[plane(i), :] * dx
        d_up, d_down = middle[i, above] - w, w - middle[i, below]
        middle_y[i, below] = slope * d_down
        middle_y[i, here] = slope * d_up
        dz = next_z(w) - w
        middle_z[plane(i - 1), :] = dz * (slope * inner)
        fz = cond_z[plane(i - 1), :] * dz
        earliest[plane(i - 1), :] = (
            decay[plane(i - 1), :] * w
            + (flux_next - flux)
            + (cond_y[i, here] * d_up - cond_y[i, below] * d_down)
            + (fz - last_z(fz))
        )
        return w_next, flux_next

    lax.fori_loop(1, cells_x + 1, earliest_plane, (middle[1, here], cond_x[plane(0), :] * dx), unroll=UNROLL)

    own.wait()
    received = inbox.at[pl.ds(0, tiles - 1)]
    pltpu.make_async_copy(received, received, piece_recv).wait()
    per_plane = cells_y // rows

    def assemble(x, carry):
        for part in range(per_plane):
            start[x + 1, pl.ds(TOP + part * rows, rows)] = inbox[holder[0, x * per_plane + part]]
        return carry

    lax.fori_loop(0, cells_x, assemble, 0, unroll=UNROLL)
    pack(START, start)
    send_edges(START, start)

    def second_plane(i, carry):
        s, flux, prod = carry
        s_next = start[i + 1, here]
        dx = s_next - s
        flux_next, prod_next = cond_x[plane(i), :] * dx, middle_x[plane(i), :] * dx
        d_up, d_down = start[i, above] - s, s - start[i, below]
        dz = next_z(s) - s
        fz, pz = cond_z[plane(i - 1), :] * dz, middle_z[plane(i - 1), :] * dz
        second[i, here] = (
            (decay[plane(i - 1), :] * s + heat[plane(i - 1), :])
            + (flux_next - flux)
            + (cond_y[i, here] * d_up - cond_y[i, below] * d_down)
            + (fz - last_z(fz))
        )
        mine[plane(i - 1), :] = (
            (prod_next + prod)
            + (middle_y[i, here] * d_up + middle_y[i, below] * d_down)
            + (pz + last_z(pz))
        )
        return s_next, flux_next, prod_next

    s = start[1, here]
    lax.fori_loop(1, cells_x + 1, second_plane, (s, cond_x[plane(0), :] * s, middle_x[plane(0), :] * s), unroll=UNROLL)

    wait_edges(START)
    for side, y, face in ((0, 0, -1), (1, cells_y - 1, cells_y - 1)):
        x = 0 if side == 0 else cells_x - 1
        second[x + 1, here] = (
            second[x + 1, here] + cond_x[plane(x + side), :] * halo_x[x_slot(START, side), :]
        )
        flat, where = edge_rows(second, y)
        faces, at = edge_rows(cond_y, face)
        flat[where, :] = flat[where, :] + faces[at, :] * halo_y[y_slot(START, side), :]
    pack(SECOND, second)
    send_edges(SECOND, second)

    def late_plane(i, carry):
        s, prod = carry
        s_next = second[i + 1, here]
        prod_next = late_x[plane(i), :] * (s_next - s)
        d_up, d_down = second[i, above] - s, s - second[i, below]
        pz = late_z[plane(i - 1), :] * (next_z(s) - s)
        mine[plane(i - 1), :] = (
            mine[plane(i - 1), :]
            + (prod_next + prod)
            + (late_y[i, here] * d_up + late_y[i, below] * d_down)
            + (pz + last_z(pz))
        )
        return s_next, prod_next

    def core_copy(index, source, target):
        return pltpu.make_async_remote_copy(
            src_ref=source,
            dst_ref=target,
            send_sem=core_send.at[index],
            recv_sem=core_recv.at[index],
            device_id=other_core,
            device_id_type=MESH,
        )

    chunk = cells_x // CHUNKS
    s = second[1, here]
    carry = (s, late_x[plane(0), :] * s)
    crossing = []
    for c in range(CHUNKS):
        carry = lax.fori_loop(1 + c * chunk, 1 + (c + 1) * chunk, late_plane, carry, unroll=UNROLL)
        part = pl.ds(c * chunk * cells_y, chunk * cells_y)
        crossing.append(core_copy(c, mine.at[part], theirs.at[part]))
        crossing[-1].start()

    wait_edges(SECOND)
    for side, face, sign in ((0, -1, -1.0), (1, cells_y - 1, 1.0)):
        x = 0 if side == 0 else cells_x
        edge_mine[pl.ds(side * cells_y, cells_y), :] = sign * (
            middle_x[plane(x), :] * halo_x[x_slot(START, side), :]
            + late_x[plane(x), :] * halo_x[x_slot(SECOND, side), :]
        )
        early, where = edge_rows(middle_y, face)
        lately, at = edge_rows(late_y, face)
        edge_mine[pl.ds(2 * cells_y + side * cells_x, cells_x), :] = sign * (
            early[where, :] * halo_y[y_slot(START, side), :]
            + lately[at, :] * halo_y[y_slot(SECOND, side), :]
        )
    crossing.append(core_copy(CHUNKS, edge_mine, edge_theirs))
    crossing[-1].start()

    sent = outbox.at[pl.ds(0, (tiles - 1) * rows)]
    pltpu.make_async_copy(sent, sent, piece_send).wait()
    for field, ref in enumerate((cond, late, middle, start, second)):
        for side in range(4):
            @pl.when(there[side])
            def _():
                edge_copy(field, ref, side).wait_send()
    for copy in crossing:
        copy.wait()


def finish_kernel(sizes, earliest, mine, theirs, edge_mine, edge_theirs, adjoint_out, gradient, total, copy_sem, part_sem):
    cells_x, cells_y = sizes
    whole = pltpu.make_async_copy(earliest, adjoint_out, copy_sem)
    whole.start()
    edge = 2 * cells_y
    chunk = cells_x // CHUNKS
    copies = []
    for c in range(CHUNKS):
        part = pl.ds(c * chunk * cells_y, chunk * cells_y)
        total[part, :] = mine[part, :] + theirs[part, :]
        for side in range(2):
            if c == side * (CHUNKS - 1):
                here = pl.ds(side * (cells_x - 1) * cells_y, cells_y)
                added = pl.ds(side * cells_y, cells_y)
                total[here, :] = total[here, :] + (edge_mine[added, :] + edge_theirs[added, :])
            here = pl.ds(c * chunk * cells_y + side * (cells_y - 1), chunk, stride=cells_y)
            added = pl.ds(edge + side * cells_x + c * chunk, chunk)
            total[here, :] = total[here, :] + (edge_mine[added, :] + edge_theirs[added, :])
        copies.append(pltpu.make_async_copy(total.at[part], gradient.at[part], part_sem.at[c]))
        copies[-1].start()
    whole.wait()
    for copy in copies:
        copy.wait()


def local(n_tx, n_ty, conductivity, cooling, source, adjoint_in, store, holder, step_index):
    cells_x, cells_y, cells_z = conductivity.shape
    _, held, _, tiles, piece = store.shape
    rows = piece // cells_z
    sizes = (n_tx, n_ty, cells_x, cells_y, cells_z, tiles, rows)
    flat = (cells_x * cells_y, cells_z)
    faces = ((cells_x + 1) * cells_y, cells_z)
    padded = (cells_x + 2, 2 * TOP + cells_y, cells_z)
    edges = (2 * cells_y + 2 * cells_x, cells_z)
    f32 = jnp.float32

    def vmem(shape):
        return pltpu.VMEM(shape, f32)

    in_smem = pl.BlockSpec(memory_space=pltpu.SMEM)
    in_hbm = pl.BlockSpec(memory_space=pltpu.HBM)
    in_vmem = pl.BlockSpec(memory_space=pltpu.VMEM)
    shaped = jax.ShapeDtypeStruct
    results = pl.pallas_call(
        functools.partial(window_kernel, sizes),
        out_shape=[shaped(flat, f32)] * 3 + [shaped(edges, f32)] * 2,
        in_specs=[in_smem] * 2 + [in_hbm] * 5,
        out_specs=[in_vmem] * 5,
        scratch_shapes=[
            vmem((held, tiles, piece)),
            vmem(flat),
            vmem((tiles, rows, cells_z)),
            *[vmem(flat)] * 4,
            *[vmem(padded)] * 5,
            *[vmem(faces), vmem(padded), vmem(flat)] * 3,
            vmem((10 * cells_y, cells_z)),
            *[vmem((10 * cells_x, cells_z))] * 2,
            pltpu.SemaphoreType.DMA((5,)),
            *[pltpu.SemaphoreType.DMA] * 3,
            *[pltpu.SemaphoreType.DMA((20,))] * 2,
            *[pltpu.SemaphoreType.DMA((CHUNKS + 1,))] * 2,
        ],
        compiler_params=pltpu.CompilerParams(
            collective_id=0, has_side_effects=True, vmem_limit_bytes=50 << 20
        ),
    )(
        step_index,
        holder,
        conductivity.reshape(flat),
        cooling.reshape(flat),
        source.reshape(flat),
        adjoint_in.reshape(flat),
        store.reshape(held, tiles, piece),
    )
    adjoint_out, gradient = pl.pallas_call(
        functools.partial(finish_kernel, (cells_x, cells_y)),
        out_shape=[shaped(flat, f32)] * 2,
        in_specs=[in_vmem] * 5,
        out_specs=[in_hbm] * 2,
        scratch_shapes=[vmem(flat), pltpu.SemaphoreType.DMA, pltpu.SemaphoreType.DMA((CHUNKS,))],
        compiler_params=pltpu.CompilerParams(vmem_limit_bytes=4 << 20),
    )(*results)
    return adjoint_out.reshape(adjoint_in.shape), gradient.reshape(conductivity.shape)


def solution(mesh):
    in_specs = (
        P("tx", "ty", None),
        P("scen", "tx", "ty", None),
        P("scen", "tx", "ty", None),
        P("scen", "tx", "ty", None),
        P("scen", None, ("tx", "ty"), None, None),
        P(("tx", "ty"), None),
        P("scen"),
    )
    out_specs = (P("scen", "tx", "ty", None), P("tx", "ty", None))
    body = functools.partial(local, mesh.shape["tx"], mesh.shape["ty"])
    return jax.shard_map(body, mesh=mesh, in_specs=in_specs, out_specs=out_specs, check_vma=False)
```

```python
import functools

import jax
import jax.numpy as jnp
from jax import lax
from jax.experimental import pallas as pl
from jax.experimental.pallas import tpu as pltpu
from jax.sharding import PartitionSpec as P

MESH = pl.DeviceIdType.MESH
step_size = 0.12
TOP = 8
COND, LATE, MIDDLE, START, SECOND = range(5)
X_LOW, X_HIGH, Y_LOW, Y_HIGH = range(4)
CHUNKS = 4
UNROLL = 8


def window_kernel(
    sizes,
    step_in, holder_in, cond_in, cool_in, heat_in, late_in, store,
    earliest, mine, theirs, edge_mine, edge_theirs,
    step, holder, saved, outbox, inbox, cond_raw, late_raw, decay, heat,
    cond, late, middle, start, second,
    cond_x, cond_y, cond_z, late_x, late_y, late_z, middle_x, middle_y, middle_z,
    halo_x, halo_y, pack_y,
    load_sem, own_sem, piece_send, piece_recv, halo_send, halo_recv, core_send, core_recv,
):
    n_tx, n_ty, cells_x, cells_y, cells_z, tiles, rows = sizes
    scen, tx, ty = lax.axis_index("scen"), lax.axis_index("tx"), lax.axis_index("ty")
    me = tx * n_ty + ty
    f32 = jnp.float32

    loads = [
        pltpu.make_async_copy(source, target, load_sem.at[i])
        for i, (source, target) in enumerate(
            [
                (step_in, step),
                (store, saved),
                (cond_in, cond_raw),
                (late_in, late_raw),
                (cool_in, decay),
                (heat_in, heat),
                (holder_in, holder),
            ]
        )
    ]
    for load in loads:
        load.start()

    def device(k):
        t = (me + k) % tiles
        return t, (scen, t // n_ty, t % n_ty)

    other_core = (1 - scen, tx, ty)
    barrier = pltpu.get_barrier_semaphore()

    def greet(k, carry):
        pl.semaphore_signal(barrier, inc=1, device_id=device(k)[1], device_id_type=MESH)
        return carry

    lax.fori_loop(1, tiles, greet, 0, unroll=True)
    pl.semaphore_signal(barrier, inc=1, device_id=other_core, device_id_type=MESH)

    def plane(x):
        return pl.ds(pl.multiple_of(x * cells_y, cells_y), cells_y)

    def piece(t):
        return pl.ds(pl.multiple_of(t * rows, rows), rows)

    here, above, below = pl.ds(TOP, cells_y), pl.ds(TOP + 1, cells_y), pl.ds(TOP - 1, cells_y)
    depth = cond.shape[1]

    def edge_rows(ref, y, first=1):
        flat = ref.reshape(ref.shape[0] * depth, cells_z)
        return flat, pl.ds(first * depth + TOP + y, cells_x, stride=depth)

    there = [tx > 0, tx < n_tx - 1, ty > 0, ty < n_ty - 1]
    neighbour = [(scen, tx - 1, ty), (scen, tx + 1, ty), (scen, tx, ty - 1), (scen, tx, ty + 1)]

    def x_slot(field, side):
        return pl.ds((field * 2 + side) * cells_y, cells_y)

    def y_slot(field, side):
        return pl.ds((field * 2 + side) * cells_x, cells_x)

    def landing(field, side):
        if side < 2:
            return halo_x.at[x_slot(field, side)]
        return halo_y.at[y_slot(field, side - 2)]

    def edge_copy(field, ref, side):
        if side < 2:
            source = ref.at[1 if side == X_LOW else cells_x, here]
        else:
            source = pack_y.at[y_slot(field, side - 2)]
        return pltpu.make_async_remote_copy(
            src_ref=source,
            dst_ref=landing(field, side ^ 1),
            send_sem=halo_send.at[field * 4 + side],
            recv_sem=halo_recv.at[field * 4 + (side ^ 1)],
            device_id=neighbour[side],
            device_id_type=MESH,
        )

    def pack(field, ref):
        for side, y in ((0, 0), (1, cells_y - 1)):
            flat, where = edge_rows(ref, y)
            pack_y[y_slot(field, side), :] = flat[where, :]

    def send_edges(field, ref):
        for side in range(4):
            @pl.when(there[side])
            def _():
                edge_copy(field, ref, side).start()

    def wait_edges(field):
        for side in range(4):
            @pl.when(there[side])
            def _():
                slot = landing(field, side)
                pltpu.make_async_copy(slot, slot, halo_recv.at[field * 4 + side]).wait()

    def unpack(field, ref):
        for side, y in ((0, -1), (1, cells_y)):
            ref[0 if side == 0 else cells_x + 1, here] = halo_x[x_slot(field, side), :]
            flat, where = edge_rows(ref, y)
            flat[where, :] = halo_y[y_slot(field, side), :]

    for side in range(4):
        @pl.when(jnp.logical_not(there[side]))
        def _():
            for field in range(5):
                slot = landing(field, side)
                slot[...] = jnp.zeros(slot.shape, f32)

    def clear(i, carry):
        for ref in (start, second):
            ref[i, pl.ds(0, TOP)] = jnp.zeros((TOP, cells_z), f32)
            ref[i, pl.ds(TOP + cells_y, TOP)] = jnp.zeros((TOP, cells_z), f32)
        return carry

    lax.fori_loop(1, cells_x + 1, clear, 0, unroll=UNROLL)
    for ref in (start, second):
        for i in (0, cells_x + 1):
            ref[i, here] = jnp.zeros((cells_y, cells_z), f32)

    loads[2].wait()
    loads[3].wait()

    def lay(x, carry):
        cond[x + 1, here] = cond_raw[plane(x), :] * (0.5 * step_size)
        late[x + 1, here] = late_raw[plane(x), :]
        return carry

    lax.fori_loop(0, cells_x, lay, 0, unroll=UNROLL)
    pack(COND, cond)
    pack(LATE, late)

    loads[0].wait()
    loads[1].wait()
    loads[6].wait()
    chosen = step[0]

    def unfold(g, carry):
        for r in range(rows):
            outbox[pl.ds(g * 8 * rows + r, 8, stride=rows), :] = saved[
                chosen, pl.ds(pl.multiple_of(g * 8, 8), 8), pl.ds(r * cells_z, cells_z)
            ]
        return carry

    lax.fori_loop(0, tiles // 8, unfold, 0)
    loads[4].wait()
    loads[5].wait()

    def scale(x, carry):
        decay[plane(x), :] = 1.0 - step_size * decay[plane(x), :]
        heat[plane(x), :] = step_size * heat[plane(x), :]
        return carry

    lax.fori_loop(0, cells_x, scale, 0, unroll=UNROLL)

    pl.semaphore_wait(barrier, tiles)

    send_edges(COND, cond)
    send_edges(LATE, late)

    def send(k, carry):
        t, target = device(k)
        pltpu.make_async_remote_copy(
            src_ref=outbox.at[piece(t)],
            dst_ref=inbox.at[me],
            send_sem=piece_send,
            recv_sem=piece_recv,
            device_id=target,
            device_id_type=MESH,
        ).start()
        return carry

    half = tiles // 2
    lax.fori_loop(1, half, send, 0)
    own = pltpu.make_async_copy(outbox.at[piece(me)], inbox.at[me], own_sem)
    own.start()

    lane = lax.broadcasted_iota(jnp.int32, (cells_y, cells_z), 1)
    inner = jnp.where(lane < cells_z - 1, f32(1), f32(0))
    slope = -0.5 * step_size

    def next_z(value):
        return pltpu.roll(value, cells_z - 1, 1)

    def last_z(value):
        return pltpu.roll(value, 1, 1)

    wait_edges(COND)
    wait_edges(LATE)
    unpack(COND, cond)
    unpack(LATE, late)

    def first_face(ref):
        return ref[1, here] - ref[0, here]

    kx = cond[0, here] + cond[1, here]
    dx = first_face(late)
    cond_x[plane(0), :] = kx
    late_x[plane(0), :] = slope * dx

    def middle_plane(i, carry):
        k, w, flux = carry
        k_next, w_next = cond[i + 1, here], late[i + 1, here]
        kx, dx = k + k_next, w_next - w
        cond_x[plane(i), :] = kx
        late_x[plane(i), :] = slope * dx
        flux_next = kx * dx
        ky_up, ky_down = k + cond[i, above], k + cond[i, below]
        d_up, d_down = late[i, above] - w, w - late[i, below]
        cond_y[i, below] = ky_down
        cond_y[i, here] = ky_up
        late_y[i, below] = slope * d_down
        late_y[i, here] = slope * d_up
        kz, dz = (k + next_z(k)) * inner, next_z(w) - w
        cond_z[plane(i - 1), :] = kz
        late_z[plane(i - 1), :] = dz * (slope * inner)
        fz = kz * dz
        middle[i, here] = (
            decay[plane(i - 1), :] * w
            + (flux_next - flux)
            + (ky_up * d_up - ky_down * d_down)
            + (fz - last_z(fz))
        )
        return k_next, w_next, flux_next

    lax.fori_loop(1, cells_x + 1, middle_plane, (cond[1, here], late[1, here], kx * dx), unroll=UNROLL)
    pack(MIDDLE, middle)
    send_edges(MIDDLE, middle)

    lax.fori_loop(half, tiles, send, 0)

    wait_edges(MIDDLE)
    unpack(MIDDLE, middle)
    dx = first_face(middle)
    middle_x[plane(0), :] = slope * dx

    def earliest_plane(i, carry):
        w, flux = carry
        w_next = middle[i + 1, here]
        dx = w_next - w
        middle_x[plane(i), :] = slope * dx
        flux_next = cond_x[plane(i), :] * dx
        d_up, d_down = middle[i, above] - w, w - middle[i, below]
        middle_y[i, below] = slope * d_down
        middle_y[i, here] = slope * d_up
        dz = next_z(w) - w
        middle_z[plane(i - 1), :] = dz * (slope * inner)
        fz = cond_z[plane(i - 1), :] * dz
        earliest[plane(i - 1), :] = (
            decay[plane(i - 1), :] * w
            + (flux_next - flux)
            + (cond_y[i, here] * d_up - cond_y[i, below] * d_down)
            + (fz - last_z(fz))
        )
        return w_next, flux_next

    lax.fori_loop(1, cells_x + 1, earliest_plane, (middle[1, here], cond_x[plane(0), :] * dx), unroll=UNROLL)

    own.wait()
    received = inbox.at[pl.ds(0, tiles - 1)]
    pltpu.make_async_copy(received, received, piece_recv).wait()
    per_plane = cells_y // rows

    def assemble(x, carry):
        for part in range(per_plane):
            start[x + 1, pl.ds(TOP + part * rows, rows)] = inbox[holder[0, x * per_plane + part]]
        return carry

    lax.fori_loop(0, cells_x, assemble, 0, unroll=UNROLL)
    pack(START, start)
    send_edges(START, start)

    def second_plane(i, carry):
        s, flux, prod = carry
        s_next = start[i + 1, here]
        dx = s_next - s
        flux_next, prod_next = cond_x[plane(i), :] * dx, middle_x[plane(i), :] * dx
        d_up, d_down = start[i, above] - s, s - start[i, below]
        dz = next_z(s) - s
        fz, pz = cond_z[plane(i - 1), :] * dz, middle_z[plane(i - 1), :] * dz
        second[i, here] = (
            (decay[plane(i - 1), :] * s + heat[plane(i - 1), :])
            + (flux_next - flux)
            + (cond_y[i, here] * d_up - cond_y[i, below] * d_down)
            + (fz - last_z(fz))
        )
        mine[plane(i - 1), :] = (
            (prod_next + prod)
            + (middle_y[i, here] * d_up + middle_y[i, below] * d_down)
            + (pz + last_z(pz))
        )
        return s_next, flux_next, prod_next

    s = start[1, here]
    lax.fori_loop(1, cells_x + 1, second_plane, (s, cond_x[plane(0), :] * s, middle_x[plane(0), :] * s), unroll=UNROLL)

    wait_edges(START)
    for side, y, face in ((0, 0, -1), (1, cells_y - 1, cells_y - 1)):
        x = 0 if side == 0 else cells_x - 1
        second[x + 1, here] = (
            second[x + 1, here] + cond_x[plane(x + side), :] * halo_x[x_slot(START, side), :]
        )
        flat, where = edge_rows(second, y)
        faces, at = edge_rows(cond_y, face)
        flat[where, :] = flat[where, :] + faces[at, :] * halo_y[y_slot(START, side), :]
    pack(SECOND, second)
    send_edges(SECOND, second)

    def late_plane(i, carry):
        s, prod = carry
        s_next = second[i + 1, here]
        prod_next = late_x[plane(i), :] * (s_next - s)
        d_up, d_down = second[i, above] - s, s - second[i, below]
        pz = late_z[plane(i - 1), :] * (next_z(s) - s)
        mine[plane(i - 1), :] = (
            mine[plane(i - 1), :]
            + (prod_next + prod)
            + (late_y[i, here] * d_up + late_y[i, below] * d_down)
            + (pz + last_z(pz))
        )
        return s_next, prod_next

    def core_copy(index, source, target):
        return pltpu.make_async_remote_copy(
            src_ref=source,
            dst_ref=target,
            send_sem=core_send.at[index],
            recv_sem=core_recv.at[index],
            device_id=other_core,
            device_id_type=MESH,
        )

    chunk = cells_x // CHUNKS
    s = second[1, here]
    carry = (s, late_x[plane(0), :] * s)
    crossing = []
    for c in range(CHUNKS):
        carry = lax.fori_loop(1 + c * chunk, 1 + (c + 1) * chunk, late_plane, carry, unroll=UNROLL)
        part = pl.ds(c * chunk * cells_y, chunk * cells_y)
        crossing.append(core_copy(c, mine.at[part], theirs.at[part]))
        crossing[-1].start()

    wait_edges(SECOND)
    for side, face, sign in ((0, -1, -1.0), (1, cells_y - 1, 1.0)):
        x = 0 if side == 0 else cells_x
        edge_mine[pl.ds(side * cells_y, cells_y), :] = sign * (
            middle_x[plane(x), :] * halo_x[x_slot(START, side), :]
            + late_x[plane(x), :] * halo_x[x_slot(SECOND, side), :]
        )
        early, where = edge_rows(middle_y, face)
        lately, at = edge_rows(late_y, face)
        edge_mine[pl.ds(2 * cells_y + side * cells_x, cells_x), :] = sign * (
            early[where, :] * halo_y[y_slot(START, side), :]
            + lately[at, :] * halo_y[y_slot(SECOND, side), :]
        )
    crossing.append(core_copy(CHUNKS, edge_mine, edge_theirs))
    crossing[-1].start()

    sent = outbox.at[pl.ds(0, (tiles - 1) * rows)]
    pltpu.make_async_copy(sent, sent, piece_send).wait()
    for field, ref in enumerate((cond, late, middle, start, second)):
        for side in range(4):
            @pl.when(there[side])
            def _():
                edge_copy(field, ref, side).wait_send()
    for copy in crossing:
        copy.wait()


def finish_kernel(sizes, earliest, mine, theirs, edge_mine, edge_theirs, adjoint_out, gradient, total, copy_sem, part_sem):
    cells_x, cells_y = sizes
    whole = pltpu.make_async_copy(earliest, adjoint_out, copy_sem)
    whole.start()
    edge = 2 * cells_y
    chunk = cells_x // CHUNKS
    copies = []
    for c in range(CHUNKS):
        part = pl.ds(c * chunk * cells_y, chunk * cells_y)
        total[part, :] = mine[part, :] + theirs[part, :]
        for side in range(2):
            if c == side * (CHUNKS - 1):
                here = pl.ds(side * (cells_x - 1) * cells_y, cells_y)
                added = pl.ds(side * cells_y, cells_y)
                total[here, :] = total[here, :] + (edge_mine[added, :] + edge_theirs[added, :])
            here = pl.ds(c * chunk * cells_y + side * (cells_y - 1), chunk, stride=cells_y)
            added = pl.ds(edge + side * cells_x + c * chunk, chunk)
            total[here, :] = total[here, :] + (edge_mine[added, :] + edge_theirs[added, :])
        copies.append(pltpu.make_async_copy(total.at[part], gradient.at[part], part_sem.at[c]))
        copies[-1].start()
    whole.wait()
    for copy in copies:
        copy.wait()


def local(n_tx, n_ty, conductivity, cooling, source, adjoint_in, store, holder, step_index):
    cells_x, cells_y, cells_z = conductivity.shape
    _, held, _, tiles, piece = store.shape
    rows = piece // cells_z
    sizes = (n_tx, n_ty, cells_x, cells_y, cells_z, tiles, rows)
    flat = (cells_x * cells_y, cells_z)
    faces = ((cells_x + 1) * cells_y, cells_z)
    padded = (cells_x + 2, 2 * TOP + cells_y, cells_z)
    edges = (2 * cells_y + 2 * cells_x, cells_z)
    f32 = jnp.float32

    def vmem(shape):
        return pltpu.VMEM(shape, f32)

    in_hbm = pl.BlockSpec(memory_space=pltpu.HBM)
    in_vmem = pl.BlockSpec(memory_space=pltpu.VMEM)
    shaped = jax.ShapeDtypeStruct
    results = pl.pallas_call(
        functools.partial(window_kernel, sizes),
        out_shape=[shaped(flat, f32)] * 3 + [shaped(edges, f32)] * 2,
        in_specs=[in_hbm] * 7,
        out_specs=[in_vmem] * 5,
        scratch_shapes=[
            pltpu.SMEM(step_index.shape, jnp.int32),
            pltpu.SMEM(holder.shape, jnp.int32),
            vmem((held, tiles, piece)),
            vmem(flat),
            vmem((tiles, rows, cells_z)),
            *[vmem(flat)] * 4,
            *[vmem(padded)] * 5,
            *[vmem(faces), vmem(padded), vmem(flat)] * 3,
            vmem((10 * cells_y, cells_z)),
            *[vmem((10 * cells_x, cells_z))] * 2,
            pltpu.SemaphoreType.DMA((7,)),
            *[pltpu.SemaphoreType.DMA] * 3,
            *[pltpu.SemaphoreType.DMA((20,))] * 2,
            *[pltpu.SemaphoreType.DMA((CHUNKS + 1,))] * 2,
        ],
        compiler_params=pltpu.CompilerParams(
            collective_id=0, has_side_effects=True, vmem_limit_bytes=50 << 20
        ),
    )(
        step_index,
        holder,
        conductivity.reshape(flat),
        cooling.reshape(flat),
        source.reshape(flat),
        adjoint_in.reshape(flat),
        store.reshape(held, tiles, piece),
    )
    adjoint_out, gradient = pl.pallas_call(
        functools.partial(finish_kernel, (cells_x, cells_y)),
        out_shape=[shaped(flat, f32)] * 2,
        in_specs=[in_vmem] * 5,
        out_specs=[in_hbm] * 2,
        scratch_shapes=[vmem(flat), pltpu.SemaphoreType.DMA, pltpu.SemaphoreType.DMA((CHUNKS,))],
        compiler_params=pltpu.CompilerParams(vmem_limit_bytes=4 << 20),
    )(*results)
    return adjoint_out.reshape(adjoint_in.shape), gradient.reshape(conductivity.shape)


def solution(mesh):
    in_specs = (
        P("tx", "ty", None),
        P("scen", "tx", "ty", None),
        P("scen", "tx", "ty", None),
        P("scen", "tx", "ty", None),
        P("scen", None, ("tx", "ty"), None, None),
        P(("tx", "ty"), None),
        P("scen"),
    )
    out_specs = (P("scen", "tx", "ty", None), P("tx", "ty", None))
    body = functools.partial(local, mesh.shape["tx"], mesh.shape["ty"])
    return jax.shard_map(body, mesh=mesh, in_specs=in_specs, out_specs=out_specs, check_vma=False)
```

```python
import functools

import jax
import jax.numpy as jnp
from jax import lax
from jax.experimental import pallas as pl
from jax.experimental.pallas import tpu as pltpu
from jax.sharding import PartitionSpec as P

MESH = pl.DeviceIdType.MESH
step_size = 0.12
TOP = 8
COND, LATE, MIDDLE, START, SECOND = range(5)
X_LOW, X_HIGH, Y_LOW, Y_HIGH = range(4)
CHUNKS = 4
UNROLL = 8


def window_kernel(
    sizes,
    step_in, holder_in, cond_in, cool_in, heat_in, late_in, store,
    earliest, mine, theirs, edge_mine, edge_theirs,
    step, holder, saved, outbox, inbox, cond_raw, late_raw, decay, heat,
    cond, late, middle, start, second,
    cond_x, cond_y, cond_z, late_x, late_y, late_z, middle_x, middle_y, middle_z,
    halo_x, halo_y, halo_corner, pack_x, pack_y, pack_corner, shift_x, shift_y,
    load_sem, own_sem, piece_send, piece_recv, halo_send, halo_recv, core_send, core_recv,
):
    n_tx, n_ty, cells_x, cells_y, cells_z, tiles, rows = sizes
    scen, tx, ty = lax.axis_index("scen"), lax.axis_index("tx"), lax.axis_index("ty")
    me = tx * n_ty + ty
    f32 = jnp.float32

    loads = [
        pltpu.make_async_copy(source, target, load_sem.at[i])
        for i, (source, target) in enumerate(
            [
                (step_in, step),
                (store, saved),
                (cond_in, cond_raw),
                (late_in, late_raw),
                (cool_in, decay),
                (heat_in, heat),
                (holder_in, holder),
            ]
        )
    ]
    for load in loads:
        load.start()

    def device(k):
        t = (me + k) % tiles
        return t, (scen, t // n_ty, t % n_ty)

    other_core = (1 - scen, tx, ty)
    barrier = pltpu.get_barrier_semaphore()

    def greet(k, carry):
        pl.semaphore_signal(barrier, inc=1, device_id=device(k)[1], device_id_type=MESH)
        return carry

    lax.fori_loop(1, tiles, greet, 0, unroll=True)
    pl.semaphore_signal(barrier, inc=1, device_id=other_core, device_id_type=MESH)

    def plane(x):
        return pl.ds(pl.multiple_of(x * cells_y, cells_y), cells_y)

    def piece(t):
        return pl.ds(pl.multiple_of(t * rows, rows), rows)

    here, above, below = pl.ds(TOP, cells_y), pl.ds(TOP + 1, cells_y), pl.ds(TOP - 1, cells_y)
    depth = cond.shape[1]

    def edge_rows(ref, y, first=1):
        flat = ref.reshape(ref.shape[0] * depth, cells_z)
        return flat, pl.ds(first * depth + TOP + y, cells_x, stride=depth)

    there = [tx > 0, tx < n_tx - 1, ty > 0, ty < n_ty - 1]
    neighbour = [(scen, tx - 1, ty), (scen, tx + 1, ty), (scen, tx, ty - 1), (scen, tx, ty + 1)]

    def x_slot(field, side):
        return pl.ds((field * 2 + side) * cells_y, cells_y)

    def y_slot(field, side):
        return pl.ds((field * 2 + side) * cells_x, cells_x)

    def landing(field, side):
        if side < 2:
            return halo_x.at[x_slot(field, side)]
        return halo_y.at[y_slot(field, side - 2)]

    def edge_copy(field, ref, side):
        if side < 2 and field == SECOND:
            source = pack_x.at[pl.ds(side * cells_y, cells_y)]
        elif side < 2:
            source = ref.at[1 if side == X_LOW else cells_x, here]
        else:
            source = pack_y.at[y_slot(field, side - 2)]
        return pltpu.make_async_remote_copy(
            src_ref=source,
            dst_ref=landing(field, side ^ 1),
            send_sem=halo_send.at[field * 4 + side],
            recv_sem=halo_recv.at[field * 4 + (side ^ 1)],
            device_id=neighbour[side],
            device_id_type=MESH,
        )

    def pack(field, ref):
        for side, y in ((0, 0), (1, cells_y - 1)):
            flat, where = edge_rows(ref, y)
            pack_y[y_slot(field, side), :] = flat[where, :]

    def send_edges(field, ref):
        for side in range(4):
            @pl.when(there[side])
            def _():
                edge_copy(field, ref, side).start()

    corners = [(0, 0), (0, 1), (1, 0), (1, 1)]
    beyond = [jnp.logical_and(there[i], there[2 + j]) for i, j in corners]

    def corner_rows(c):
        return pl.ds(c * 8, 8)

    def corner_copy(c):
        i, j = corners[c]
        return pltpu.make_async_remote_copy(
            src_ref=pack_corner.at[corner_rows(c)],
            dst_ref=halo_corner.at[corner_rows(3 - c)],
            send_sem=halo_send.at[20 + c],
            recv_sem=halo_recv.at[20 + 3 - c],
            device_id=(scen, tx + 2 * i - 1, ty + 2 * j - 1),
            device_id_type=MESH,
        )

    def wait_edges(field):
        for side in range(4):
            @pl.when(there[side])
            def _():
                slot = landing(field, side)
                pltpu.make_async_copy(slot, slot, halo_recv.at[field * 4 + side]).wait()

    def unpack(field, ref):
        for side, y in ((0, -1), (1, cells_y)):
            ref[0 if side == 0 else cells_x + 1, here] = halo_x[x_slot(field, side), :]
            flat, where = edge_rows(ref, y)
            flat[where, :] = halo_y[y_slot(field, side), :]

    for side in range(4):
        @pl.when(jnp.logical_not(there[side]))
        def _():
            for field in range(5):
                slot = landing(field, side)
                slot[...] = jnp.zeros(slot.shape, f32)

    for c in range(4):
        @pl.when(jnp.logical_not(beyond[c]))
        def _():
            halo_corner[corner_rows(c), :] = jnp.zeros((8, cells_z), f32)

    pack_corner[...] = jnp.zeros(pack_corner.shape, f32)
    shift_x[...] = jnp.zeros(shift_x.shape, f32)
    shift_y[...] = jnp.zeros(shift_y.shape, f32)

    def clear(i, carry):
        for ref in (start, second):
            ref[i, pl.ds(0, TOP)] = jnp.zeros((TOP, cells_z), f32)
            ref[i, pl.ds(TOP + cells_y, TOP)] = jnp.zeros((TOP, cells_z), f32)
        return carry

    lax.fori_loop(1, cells_x + 1, clear, 0, unroll=UNROLL)
    for ref in (start, second):
        for i in (0, cells_x + 1):
            ref[i, here] = jnp.zeros((cells_y, cells_z), f32)

    loads[2].wait()
    loads[3].wait()

    def lay(x, carry):
        cond[x + 1, here] = cond_raw[plane(x), :] * (0.5 * step_size)
        late[x + 1, here] = late_raw[plane(x), :]
        return carry

    lax.fori_loop(0, cells_x, lay, 0, unroll=UNROLL)
    pack(COND, cond)
    pack(LATE, late)

    loads[0].wait()
    loads[1].wait()
    loads[6].wait()
    chosen = step[0]

    def unfold(g, carry):
        for r in range(rows):
            outbox[pl.ds(g * 8 * rows + r, 8, stride=rows), :] = saved[
                chosen, pl.ds(pl.multiple_of(g * 8, 8), 8), pl.ds(r * cells_z, cells_z)
            ]
        return carry

    lax.fori_loop(0, tiles // 8, unfold, 0)
    loads[4].wait()
    loads[5].wait()

    def scale(x, carry):
        decay[plane(x), :] = 1.0 - step_size * decay[plane(x), :]
        heat[plane(x), :] = step_size * heat[plane(x), :]
        return carry

    lax.fori_loop(0, cells_x, scale, 0, unroll=UNROLL)

    pl.semaphore_wait(barrier, tiles)

    send_edges(COND, cond)
    send_edges(LATE, late)

    def send(k, carry):
        t, target = device(k)
        pltpu.make_async_remote_copy(
            src_ref=outbox.at[piece(t)],
            dst_ref=inbox.at[me],
            send_sem=piece_send,
            recv_sem=piece_recv,
            device_id=target,
            device_id_type=MESH,
        ).start()
        return carry

    half = tiles // 2
    lax.fori_loop(1, half, send, 0)
    own = pltpu.make_async_copy(outbox.at[piece(me)], inbox.at[me], own_sem)
    own.start()

    lane = lax.broadcasted_iota(jnp.int32, (cells_y, cells_z), 1)
    inner = jnp.where(lane < cells_z - 1, f32(1), f32(0))
    slope = -0.5 * step_size

    def next_z(value):
        return pltpu.roll(value, cells_z - 1, 1)

    def last_z(value):
        return pltpu.roll(value, 1, 1)

    wait_edges(COND)
    wait_edges(LATE)
    unpack(COND, cond)
    unpack(LATE, late)

    def first_face(ref):
        return ref[1, here] - ref[0, here]

    kx = cond[0, here] + cond[1, here]
    dx = first_face(late)
    cond_x[plane(0), :] = kx
    late_x[plane(0), :] = slope * dx

    def middle_plane(i, carry):
        k, w, flux = carry
        k_next, w_next = cond[i + 1, here], late[i + 1, here]
        kx, dx = k + k_next, w_next - w
        cond_x[plane(i), :] = kx
        late_x[plane(i), :] = slope * dx
        flux_next = kx * dx
        ky_up, ky_down = k + cond[i, above], k + cond[i, below]
        d_up, d_down = late[i, above] - w, w - late[i, below]
        cond_y[i, below] = ky_down
        cond_y[i, here] = ky_up
        late_y[i, below] = slope * d_down
        late_y[i, here] = slope * d_up
        kz, dz = (k + next_z(k)) * inner, next_z(w) - w
        cond_z[plane(i - 1), :] = kz
        late_z[plane(i - 1), :] = dz * (slope * inner)
        fz = kz * dz
        middle[i, here] = (
            decay[plane(i - 1), :] * w
            + (flux_next - flux)
            + (ky_up * d_up - ky_down * d_down)
            + (fz - last_z(fz))
        )
        return k_next, w_next, flux_next

    lax.fori_loop(1, cells_x + 1, middle_plane, (cond[1, here], late[1, here], kx * dx), unroll=UNROLL)
    pack(MIDDLE, middle)
    send_edges(MIDDLE, middle)

    lax.fori_loop(half, tiles, send, 0)

    wait_edges(MIDDLE)
    unpack(MIDDLE, middle)
    dx = first_face(middle)
    middle_x[plane(0), :] = slope * dx

    def earliest_plane(i, carry):
        w, flux = carry
        w_next = middle[i + 1, here]
        dx = w_next - w
        middle_x[plane(i), :] = slope * dx
        flux_next = cond_x[plane(i), :] * dx
        d_up, d_down = middle[i, above] - w, w - middle[i, below]
        middle_y[i, below] = slope * d_down
        middle_y[i, here] = slope * d_up
        dz = next_z(w) - w
        middle_z[plane(i - 1), :] = dz * (slope * inner)
        fz = cond_z[plane(i - 1), :] * dz
        earliest[plane(i - 1), :] = (
            decay[plane(i - 1), :] * w
            + (flux_next - flux)
            + (cond_y[i, here] * d_up - cond_y[i, below] * d_down)
            + (fz - last_z(fz))
        )
        return w_next, flux_next

    lax.fori_loop(1, cells_x + 1, earliest_plane, (middle[1, here], cond_x[plane(0), :] * dx), unroll=UNROLL)

    own.wait()
    received = inbox.at[pl.ds(0, tiles - 1)]
    pltpu.make_async_copy(received, received, piece_recv).wait()
    per_plane = cells_y // rows

    def assemble(x, carry):
        for part in range(per_plane):
            start[x + 1, pl.ds(TOP + part * rows, rows)] = inbox[holder[0, x * per_plane + part]]
        return carry

    lax.fori_loop(0, cells_x, assemble, 0, unroll=UNROLL)
    pack(START, start)
    send_edges(START, start)

    def row(ref, y, first=1):
        flat, where = edge_rows(ref, y, first)
        return flat[where, :]

    def flat_row(ref, y, first=0):
        return ref[pl.ds(first * cells_y + y, cells_x, stride=cells_y), :]

    def advanced(s, x_next, x_last, y_next, y_last, kx_next, kx_last, ky_next, ky_last, kz, a, b):
        fz = kz * (next_z(s) - s)
        return (
            (a * s + b)
            + (kx_next * (x_next - s) - kx_last * (s - x_last))
            + (ky_next * (y_next - s) - ky_last * (s - y_last))
            + (fz - last_z(fz))
        )

    for side, i, y in ((0, 1, 0), (1, cells_x, cells_y - 1)):
        at = plane(i - 1)
        pack_x[pl.ds(side * cells_y, cells_y), :] = advanced(
            start[i, here], start[i + 1, here], start[i - 1, here], start[i, above], start[i, below],
            cond_x[plane(i), :], cond_x[at, :], cond_y[i, here], cond_y[i, below],
            cond_z[at, :], decay[at, :], heat[at, :],
        )
        pack_y[y_slot(SECOND, side), :] = advanced(
            row(start, y), row(start, y, 2), row(start, y, 0), row(start, y + 1), row(start, y - 1),
            flat_row(cond_x, y, 1), flat_row(cond_x, y), row(cond_y, y), row(cond_y, y - 1),
            flat_row(cond_z, y), flat_row(decay, y), flat_row(heat, y),
        )
    for c, (i, j) in enumerate(corners):
        x, y = i * (cells_x - 1), j * (cells_y - 1)
        value = start[x + 1, pl.ds(TOP + y, 1)]
        pack_corner[pl.ds(c * 8, 1), :] = value * cond_y[x + 1, pl.ds(TOP + y - 1 + j, 1)]
        pack_corner[pl.ds(c * 8 + 1, 1), :] = value * cond_x[pl.ds((x + i) * cells_y + y, 1), :]
    send_edges(SECOND, second)
    for c in range(4):
        @pl.when(beyond[c])
        def _():
            corner_copy(c).start()

    def second_plane(i, carry):
        s, flux, prod = carry
        s_next = start[i + 1, here]
        dx = s_next - s
        flux_next, prod_next = cond_x[plane(i), :] * dx, middle_x[plane(i), :] * dx
        d_up, d_down = start[i, above] - s, s - start[i, below]
        dz = next_z(s) - s
        fz, pz = cond_z[plane(i - 1), :] * dz, middle_z[plane(i - 1), :] * dz
        second[i, here] = (
            (decay[plane(i - 1), :] * s + heat[plane(i - 1), :])
            + (flux_next - flux)
            + (cond_y[i, here] * d_up - cond_y[i, below] * d_down)
            + (fz - last_z(fz))
        )
        mine[plane(i - 1), :] = (
            (prod_next + prod)
            + (middle_y[i, here] * d_up + middle_y[i, below] * d_down)
            + (pz + last_z(pz))
        )
        return s_next, flux_next, prod_next

    s = start[1, here]
    lax.fori_loop(1, cells_x + 1, second_plane, (s, cond_x[plane(0), :] * s, middle_x[plane(0), :] * s), unroll=UNROLL)

    def late_plane(i, carry):
        s, prod = carry
        s_next = second[i + 1, here]
        prod_next = late_x[plane(i), :] * (s_next - s)
        d_up, d_down = second[i, above] - s, s - second[i, below]
        pz = late_z[plane(i - 1), :] * (next_z(s) - s)
        mine[plane(i - 1), :] = (
            mine[plane(i - 1), :]
            + (prod_next + prod)
            + (late_y[i, here] * d_up + late_y[i, below] * d_down)
            + (pz + last_z(pz))
        )
        return s_next, prod_next

    def core_copy(index, source, target):
        return pltpu.make_async_remote_copy(
            src_ref=source,
            dst_ref=target,
            send_sem=core_send.at[index],
            recv_sem=core_recv.at[index],
            device_id=other_core,
            device_id_type=MESH,
        )

    chunk = cells_x // CHUNKS
    s = second[1, here]
    carry = (s, late_x[plane(0), :] * s)
    crossing = []
    for c in range(CHUNKS):
        carry = lax.fori_loop(1 + c * chunk, 1 + (c + 1) * chunk, late_plane, carry, unroll=UNROLL)
        part = pl.ds(c * chunk * cells_y, chunk * cells_y)
        crossing.append(core_copy(c, mine.at[part], theirs.at[part]))
        crossing[-1].start()

    wait_edges(START)
    wait_edges(SECOND)
    for c in range(4):
        @pl.when(beyond[c])
        def _():
            slot = halo_corner.at[corner_rows(c)]
            pltpu.make_async_copy(slot, slot, halo_recv.at[20 + c]).wait()

    known = [jnp.where(exists, f32(1), f32(0)) for exists in there]

    def added(add, add_next, add_last, inner_last, inner_next, up, down, z):
        pz = z * (next_z(add) - add)
        return (
            add * (inner_last - inner_next)
            + (up * (add_next - add) + down * (add - add_last))
            + (pz + last_z(pz))
        )

    for side, sign in ((0, -1.0), (1, 1.0)):
        i, face, inward = (1, 0, 1) if side == 0 else (cells_x, cells_x, cells_x - 1)
        near = x_slot(START, side)
        far = x_slot(SECOND, side)
        k = cond_x[plane(face), :]
        add = k * halo_x[near, :]
        halo_x[far, :] = halo_x[far, :] + known[side] * (k * start[i, here])
        for j in range(2):
            at = pl.ds((SECOND * 2 + side) * cells_y + j * (cells_y - 1), 1)
            halo_x[at, :] = halo_x[at, :] + halo_corner[pl.ds((side * 2 + j) * 8, 1), :]
        base = side * (cells_y + 2 * TOP) + TOP
        shift_x[pl.ds(base, cells_y), :] = add
        edge_mine[pl.ds(side * cells_y, cells_y), :] = added(
            add, shift_x[pl.ds(base + 1, cells_y), :], shift_x[pl.ds(base - 1, cells_y), :],
            late_x[plane(i - 1), :], late_x[plane(i), :],
            late_y[i, here], late_y[i, below], late_z[plane(i - 1), :],
        ) + sign * (
            middle_x[plane(face), :] * halo_x[near, :] + late_x[plane(face), :] * halo_x[far, :]
        )
        edge_mine[pl.ds((2 + side) * cells_y, cells_y), :] = sign * (add * late_x[plane(inward), :])

        y, face, inward = (0, -1, 0) if side == 0 else (cells_y - 1, cells_y - 1, cells_y - 2)
        near = y_slot(START, side)
        far = y_slot(SECOND, side)
        k = row(cond_y, face)
        add = k * halo_y[near, :]
        halo_y[far, :] = halo_y[far, :] + known[2 + side] * (k * row(start, y))
        for j in range(2):
            at = pl.ds((SECOND * 2 + side) * cells_x + j * (cells_x - 1), 1)
            halo_y[at, :] = halo_y[at, :] + halo_corner[pl.ds((j * 2 + side) * 8 + 1, 1), :]
        base = side * (cells_x + 2 * TOP) + TOP
        shift_y[pl.ds(base, cells_x), :] = add
        edges_y = 4 * cells_y + side * cells_x
        edge_mine[pl.ds(edges_y, cells_x), :] = added(
            add, shift_y[pl.ds(base + 1, cells_x), :], shift_y[pl.ds(base - 1, cells_x), :],
            row(late_y, y - 1), row(late_y, y),
            flat_row(late_x, y, 1), flat_row(late_x, y), flat_row(late_z, y),
        ) + sign * (row(middle_y, face) * halo_y[near, :] + row(late_y, face) * halo_y[far, :])
        edge_mine[pl.ds(edges_y + 2 * cells_x, cells_x), :] = sign * (add * row(late_y, inward))
    crossing.append(core_copy(CHUNKS, edge_mine, edge_theirs))
    crossing[-1].start()

    sent = outbox.at[pl.ds(0, (tiles - 1) * rows)]
    pltpu.make_async_copy(sent, sent, piece_send).wait()
    for field, ref in enumerate((cond, late, middle, start, second)):
        for side in range(4):
            @pl.when(there[side])
            def _():
                edge_copy(field, ref, side).wait_send()
    for c in range(4):
        @pl.when(beyond[c])
        def _():
            corner_copy(c).wait_send()
    for copy in crossing:
        copy.wait()


def finish_kernel(sizes, earliest, mine, theirs, edge_mine, edge_theirs, adjoint_out, gradient, total, copy_sem, part_sem):
    cells_x, cells_y = sizes
    whole = pltpu.make_async_copy(earliest, adjoint_out, copy_sem)
    whole.start()
    chunk = cells_x // CHUNKS
    copies = []
    for c in range(CHUNKS):
        part = pl.ds(c * chunk * cells_y, chunk * cells_y)
        total[part, :] = mine[part, :] + theirs[part, :]
        for depth in range(2):
            for side in range(2):
                if c == side * (CHUNKS - 1):
                    x = cells_x - 1 - depth if side else depth
                    here = pl.ds(x * cells_y, cells_y)
                    added = pl.ds((2 * depth + side) * cells_y, cells_y)
                    total[here, :] = total[here, :] + (edge_mine[added, :] + edge_theirs[added, :])
                y = cells_y - 1 - depth if side else depth
                here = pl.ds(c * chunk * cells_y + y, chunk, stride=cells_y)
                added = pl.ds(4 * cells_y + (2 * depth + side) * cells_x + c * chunk, chunk)
                total[here, :] = total[here, :] + (edge_mine[added, :] + edge_theirs[added, :])
        copies.append(pltpu.make_async_copy(total.at[part], gradient.at[part], part_sem.at[c]))
        copies[-1].start()
    whole.wait()
    for copy in copies:
        copy.wait()


def local(n_tx, n_ty, conductivity, cooling, source, adjoint_in, store, holder, step_index):
    cells_x, cells_y, cells_z = conductivity.shape
    _, held, _, tiles, piece = store.shape
    rows = piece // cells_z
    sizes = (n_tx, n_ty, cells_x, cells_y, cells_z, tiles, rows)
    flat = (cells_x * cells_y, cells_z)
    faces = ((cells_x + 1) * cells_y, cells_z)
    padded = (cells_x + 2, 2 * TOP + cells_y, cells_z)
    edges = (4 * cells_y + 4 * cells_x, cells_z)
    f32 = jnp.float32

    def vmem(shape):
        return pltpu.VMEM(shape, f32)

    in_hbm = pl.BlockSpec(memory_space=pltpu.HBM)
    in_vmem = pl.BlockSpec(memory_space=pltpu.VMEM)
    shaped = jax.ShapeDtypeStruct
    results = pl.pallas_call(
        functools.partial(window_kernel, sizes),
        out_shape=[shaped(flat, f32)] * 3 + [shaped(edges, f32)] * 2,
        in_specs=[in_hbm] * 7,
        out_specs=[in_vmem] * 5,
        scratch_shapes=[
            pltpu.SMEM(step_index.shape, jnp.int32),
            pltpu.SMEM(holder.shape, jnp.int32),
            vmem((held, tiles, piece)),
            vmem(flat),
            vmem((tiles, rows, cells_z)),
            *[vmem(flat)] * 4,
            *[vmem(padded)] * 5,
            *[vmem(faces), vmem(padded), vmem(flat)] * 3,
            vmem((10 * cells_y, cells_z)),
            vmem((10 * cells_x, cells_z)),
            vmem((32, cells_z)),
            vmem((2 * cells_y, cells_z)),
            vmem((10 * cells_x, cells_z)),
            vmem((32, cells_z)),
            vmem((2 * (cells_y + 2 * TOP), cells_z)),
            vmem((2 * (cells_x + 2 * TOP), cells_z)),
            pltpu.SemaphoreType.DMA((7,)),
            *[pltpu.SemaphoreType.DMA] * 3,
            *[pltpu.SemaphoreType.DMA((24,))] * 2,
            *[pltpu.SemaphoreType.DMA((CHUNKS + 1,))] * 2,
        ],
        compiler_params=pltpu.CompilerParams(
            collective_id=0, has_side_effects=True, vmem_limit_bytes=50 << 20
        ),
    )(
        step_index,
        holder,
        conductivity.reshape(flat),
        cooling.reshape(flat),
        source.reshape(flat),
        adjoint_in.reshape(flat),
        store.reshape(held, tiles, piece),
    )
    adjoint_out, gradient = pl.pallas_call(
        functools.partial(finish_kernel, (cells_x, cells_y)),
        out_shape=[shaped(flat, f32)] * 2,
        in_specs=[in_vmem] * 5,
        out_specs=[in_hbm] * 2,
        scratch_shapes=[vmem(flat), pltpu.SemaphoreType.DMA, pltpu.SemaphoreType.DMA((CHUNKS,))],
        compiler_params=pltpu.CompilerParams(vmem_limit_bytes=4 << 20),
    )(*results)
    return adjoint_out.reshape(adjoint_in.shape), gradient.reshape(conductivity.shape)


def solution(mesh):
    in_specs = (
        P("tx", "ty", None),
        P("scen", "tx", "ty", None),
        P("scen", "tx", "ty", None),
        P("scen", "tx", "ty", None),
        P("scen", None, ("tx", "ty"), None, None),
        P(("tx", "ty"), None),
        P("scen"),
    )
    out_specs = (P("scen", "tx", "ty", None), P("tx", "ty", None))
    body = functools.partial(local, mesh.shape["tx"], mesh.shape["ty"])
    return jax.shard_map(body, mesh=mesh, in_specs=in_specs, out_specs=out_specs, check_vma=False)
```

```python
import functools

import jax
import jax.numpy as jnp
from jax import lax
from jax.experimental import pallas as pl
from jax.experimental.pallas import tpu as pltpu
from jax.sharding import PartitionSpec as P

MESH = pl.DeviceIdType.MESH
step_size = 0.12
TOP = 8
COND, LATE, MIDDLE, START, SECOND = range(5)
X_LOW, X_HIGH, Y_LOW, Y_HIGH = range(4)
CHUNKS = 4
UNROLL = 8


def window_kernel(
    sizes,
    step_in, holder_in, cond_in, cool_in, heat_in, late_in, store,
    earliest, mine, theirs, edge_mine, edge_theirs,
    step, holder, saved, outbox, inbox, cond_raw, late_raw, decay, heat,
    cond, late, middle, start, second,
    cond_x, cond_y, cond_z, late_x, late_y, late_z, middle_x, middle_y, middle_z,
    halo_x, halo_y, halo_corner, pack_x, pack_y, pack_corner, shift_x, shift_y,
    load_sem, own_sem, piece_send, piece_recv, halo_send, halo_recv, core_send, core_recv,
):
    n_tx, n_ty, cells_x, cells_y, cells_z, tiles, rows = sizes
    scen, tx, ty = lax.axis_index("scen"), lax.axis_index("tx"), lax.axis_index("ty")
    me = tx * n_ty + ty
    f32 = jnp.float32

    loads = [
        pltpu.make_async_copy(source, target, load_sem.at[i])
        for i, (source, target) in enumerate(
            [
                (step_in, step),
                (store, saved),
                (cond_in, cond_raw),
                (late_in, late_raw),
                (cool_in, decay.at[pl.ds(0, cells_x * cells_y)]),
                (heat_in, heat.at[pl.ds(0, cells_x * cells_y)]),
                (holder_in, holder),
            ]
        )
    ]
    for load in loads:
        load.start()

    def device(k):
        t = (me + k) % tiles
        return t, (scen, t // n_ty, t % n_ty)

    other_core = (1 - scen, tx, ty)
    barrier = pltpu.get_barrier_semaphore()

    def greet(k, carry):
        pl.semaphore_signal(barrier, inc=1, device_id=device(k)[1], device_id_type=MESH)
        return carry

    lax.fori_loop(1, tiles, greet, 0, unroll=True)
    pl.semaphore_signal(barrier, inc=1, device_id=other_core, device_id_type=MESH)

    def plane(x):
        return pl.ds(pl.multiple_of(x * cells_y, cells_y), cells_y)

    def piece(t):
        return pl.ds(pl.multiple_of(t * rows, rows), rows)

    here, above, below = pl.ds(TOP, cells_y), pl.ds(TOP + 1, cells_y), pl.ds(TOP - 1, cells_y)
    depth = cond.shape[1]

    def edge_rows(ref, y, first=1):
        flat = ref.reshape(ref.shape[0] * depth, cells_z)
        return flat, pl.ds(first * depth + TOP + y, cells_x, stride=depth)

    there = [tx > 0, tx < n_tx - 1, ty > 0, ty < n_ty - 1]
    neighbour = [(scen, tx - 1, ty), (scen, tx + 1, ty), (scen, tx, ty - 1), (scen, tx, ty + 1)]

    def x_slot(field, side):
        return pl.ds((field * 2 + side) * cells_y, cells_y)

    def y_slot(field, side):
        return pl.ds((field * 2 + side) * cells_x, cells_x)

    def landing(field, side):
        if side < 2:
            return halo_x.at[x_slot(field, side)]
        return halo_y.at[y_slot(field, side - 2)]

    def edge_copy(field, ref, side):
        if side < 2 and field == SECOND:
            source = pack_x.at[pl.ds(side * cells_y, cells_y)]
        elif side < 2:
            source = ref.at[1 if side == X_LOW else cells_x, here]
        else:
            source = pack_y.at[y_slot(field, side - 2)]
        return pltpu.make_async_remote_copy(
            src_ref=source,
            dst_ref=landing(field, side ^ 1),
            send_sem=halo_send.at[field * 4 + side],
            recv_sem=halo_recv.at[field * 4 + (side ^ 1)],
            device_id=neighbour[side],
            device_id_type=MESH,
        )

    def pack(field, ref):
        for side, y in ((0, 0), (1, cells_y - 1)):
            flat, where = edge_rows(ref, y)
            pack_y[y_slot(field, side), :] = flat[where, :]

    def send_edges(field, ref):
        for side in range(4):
            @pl.when(there[side])
            def _():
                edge_copy(field, ref, side).start()

    corners = [(0, 0), (0, 1), (1, 0), (1, 1)]
    beyond = [jnp.logical_and(there[i], there[2 + j]) for i, j in corners]

    def corner_rows(c):
        return pl.ds(c * 8, 8)

    def corner_copy(c):
        i, j = corners[c]
        return pltpu.make_async_remote_copy(
            src_ref=pack_corner.at[corner_rows(c)],
            dst_ref=halo_corner.at[corner_rows(3 - c)],
            send_sem=halo_send.at[20 + c],
            recv_sem=halo_recv.at[20 + 3 - c],
            device_id=(scen, tx + 2 * i - 1, ty + 2 * j - 1),
            device_id_type=MESH,
        )

    def wait_edges(field):
        for side in range(4):
            @pl.when(there[side])
            def _():
                slot = landing(field, side)
                pltpu.make_async_copy(slot, slot, halo_recv.at[field * 4 + side]).wait()

    def unpack(field, ref):
        for side, y in ((0, -1), (1, cells_y)):
            ref[0 if side == 0 else cells_x + 1, here] = halo_x[x_slot(field, side), :]
            flat, where = edge_rows(ref, y)
            flat[where, :] = halo_y[y_slot(field, side), :]

    for side in range(4):
        @pl.when(jnp.logical_not(there[side]))
        def _():
            for field in range(5):
                slot = landing(field, side)
                slot[...] = jnp.zeros(slot.shape, f32)

    for c in range(4):
        @pl.when(jnp.logical_not(beyond[c]))
        def _():
            halo_corner[corner_rows(c), :] = jnp.zeros((8, cells_z), f32)

    pack_corner[...] = jnp.zeros(pack_corner.shape, f32)
    shift_x[...] = jnp.zeros(shift_x.shape, f32)
    shift_y[...] = jnp.zeros(shift_y.shape, f32)

    def clear(i, carry):
        for ref in (start, second):
            ref[i, pl.ds(0, TOP)] = jnp.zeros((TOP, cells_z), f32)
            ref[i, pl.ds(TOP + cells_y, TOP)] = jnp.zeros((TOP, cells_z), f32)
        return carry

    lax.fori_loop(1, cells_x + 1, clear, 0, unroll=UNROLL)
    for ref in (start, second):
        for i in (0, cells_x + 1):
            ref[i, here] = jnp.zeros((cells_y, cells_z), f32)

    loads[2].wait()
    loads[3].wait()

    def lay(x, carry):
        cond[x + 1, here] = cond_raw[plane(x), :] * (0.5 * step_size)
        late[x + 1, here] = late_raw[plane(x), :]
        return carry

    lax.fori_loop(0, cells_x, lay, 0, unroll=UNROLL)
    pack(COND, cond)
    pack(LATE, late)

    loads[0].wait()
    loads[1].wait()
    loads[6].wait()
    chosen = step[0]

    def unfold(g, carry):
        for r in range(rows):
            outbox[pl.ds(g * 8 * rows + r, 8, stride=rows), :] = saved[
                chosen, pl.ds(pl.multiple_of(g * 8, 8), 8), pl.ds(r * cells_z, cells_z)
            ]
        return carry

    lax.fori_loop(0, tiles // 8, unfold, 0)
    loads[4].wait()
    loads[5].wait()

    def scale(x, carry):
        decay[plane(x), :] = 1.0 - step_size * decay[plane(x), :]
        heat[plane(x), :] = step_size * heat[plane(x), :]
        return carry

    lax.fori_loop(0, cells_x, scale, 0, unroll=UNROLL)

    pl.semaphore_wait(barrier, tiles)

    send_edges(COND, cond)
    send_edges(LATE, late)

    def send(k, carry):
        t, target = device(k)
        pltpu.make_async_remote_copy(
            src_ref=outbox.at[piece(t)],
            dst_ref=inbox.at[me],
            send_sem=piece_send,
            recv_sem=piece_recv,
            device_id=target,
            device_id_type=MESH,
        ).start()
        return carry

    half = tiles // 2
    lax.fori_loop(1, half, send, 0)
    own = pltpu.make_async_copy(outbox.at[piece(me)], inbox.at[me], own_sem)
    own.start()

    lane = lax.broadcasted_iota(jnp.int32, (cells_y, cells_z), 1)
    inner = jnp.where(lane < cells_z - 1, f32(1), f32(0))
    slope = -0.5 * step_size

    def next_z(value):
        return pltpu.roll(value, cells_z - 1, 1)

    def last_z(value):
        return pltpu.roll(value, 1, 1)

    wait_edges(COND)
    wait_edges(LATE)
    unpack(COND, cond)
    unpack(LATE, late)

    def first_face(ref):
        return ref[1, here] - ref[0, here]

    kx = cond[0, here] + cond[1, here]
    dx = first_face(late)
    cond_x[plane(0), :] = kx
    late_x[plane(0), :] = slope * dx

    def middle_plane(i, carry):
        k, w, flux = carry
        k_next, w_next = cond[i + 1, here], late[i + 1, here]
        kx, dx = k + k_next, w_next - w
        cond_x[plane(i), :] = kx
        late_x[plane(i), :] = slope * dx
        flux_next = kx * dx
        ky_up, ky_down = k + cond[i, above], k + cond[i, below]
        d_up, d_down = late[i, above] - w, w - late[i, below]
        cond_y[i, below] = ky_down
        cond_y[i, here] = ky_up
        late_y[i, below] = slope * d_down
        late_y[i, here] = slope * d_up
        kz, dz = (k + next_z(k)) * inner, next_z(w) - w
        cond_z[plane(i - 1), :] = kz
        late_z[plane(i - 1), :] = dz * (slope * inner)
        fz = kz * dz
        middle[i, here] = (
            decay[plane(i - 1), :] * w
            + (flux_next - flux)
            + (ky_up * d_up - ky_down * d_down)
            + (fz - last_z(fz))
        )
        return k_next, w_next, flux_next

    lax.fori_loop(1, cells_x + 1, middle_plane, (cond[1, here], late[1, here], kx * dx), unroll=UNROLL)
    pack(MIDDLE, middle)
    send_edges(MIDDLE, middle)

    lax.fori_loop(half, tiles, send, 0)

    wait_edges(MIDDLE)
    unpack(MIDDLE, middle)
    dx = first_face(middle)
    middle_x[plane(0), :] = slope * dx

    def earliest_plane(i, carry):
        w, flux = carry
        w_next = middle[i + 1, here]
        dx = w_next - w
        middle_x[plane(i), :] = slope * dx
        flux_next = cond_x[plane(i), :] * dx
        d_up, d_down = middle[i, above] - w, w - middle[i, below]
        middle_y[i, below] = slope * d_down
        middle_y[i, here] = slope * d_up
        dz = next_z(w) - w
        middle_z[plane(i - 1), :] = dz * (slope * inner)
        fz = cond_z[plane(i - 1), :] * dz
        earliest[plane(i - 1), :] = (
            decay[plane(i - 1), :] * w
            + (flux_next - flux)
            + (cond_y[i, here] * d_up - cond_y[i, below] * d_down)
            + (fz - last_z(fz))
        )
        return w_next, flux_next

    lax.fori_loop(1, cells_x + 1, earliest_plane, (middle[1, here], cond_x[plane(0), :] * dx), unroll=UNROLL)

    own.wait()
    received = inbox.at[pl.ds(0, tiles - 1)]
    pltpu.make_async_copy(received, received, piece_recv).wait()
    per_plane = cells_y // rows

    def assemble(x, carry):
        for part in range(per_plane):
            start[x + 1, pl.ds(TOP + part * rows, rows)] = inbox[holder[0, x * per_plane + part]]
        return carry

    lax.fori_loop(0, cells_x, assemble, 0, unroll=UNROLL)
    pack(START, start)
    send_edges(START, start)

    def row(ref, y, first=1):
        flat, where = edge_rows(ref, y, first)
        return flat[where, :]

    def flat_row(ref, y, first=0):
        return ref[pl.ds(first * cells_y + y, cells_x, stride=cells_y), :]

    def advanced(s, x_next, x_last, y_next, y_last, kx_next, kx_last, ky_next, ky_last, kz, a, b):
        fz = kz * (next_z(s) - s)
        return (
            (a * s + b)
            + (kx_next * (x_next - s) - kx_last * (s - x_last))
            + (ky_next * (y_next - s) - ky_last * (s - y_last))
            + (fz - last_z(fz))
        )

    for side, i, y in ((0, 1, 0), (1, cells_x, cells_y - 1)):
        at = plane(i - 1)
        pack_x[pl.ds(side * cells_y, cells_y), :] = advanced(
            start[i, here], start[i + 1, here], start[i - 1, here], start[i, above], start[i, below],
            cond_x[plane(i), :], cond_x[at, :], cond_y[i, here], cond_y[i, below],
            cond_z[at, :], decay[at, :], heat[at, :],
        )
        pack_y[y_slot(SECOND, side), :] = advanced(
            row(start, y), row(start, y, 2), row(start, y, 0), row(start, y + 1), row(start, y - 1),
            flat_row(cond_x, y, 1), flat_row(cond_x, y), row(cond_y, y), row(cond_y, y - 1),
            flat_row(cond_z, y), flat_row(decay, y), flat_row(heat, y),
        )
    for c, (i, j) in enumerate(corners):
        x, y = i * (cells_x - 1), j * (cells_y - 1)
        value = start[x + 1, pl.ds(TOP + y, 1)]
        pack_corner[pl.ds(c * 8, 1), :] = value * cond_y[x + 1, pl.ds(TOP + y - 1 + j, 1)]
        pack_corner[pl.ds(c * 8 + 1, 1), :] = value * cond_x[pl.ds((x + i) * cells_y + y, 1), :]
    send_edges(SECOND, second)
    for c in range(4):
        @pl.when(beyond[c])
        def _():
            corner_copy(c).start()

    def second_plane(i, carry):
        s, flux, prod = carry
        s_next = start[i + 1, here]
        dx = s_next - s
        flux_next, prod_next = cond_x[plane(i), :] * dx, middle_x[plane(i), :] * dx
        d_up, d_down = start[i, above] - s, s - start[i, below]
        dz = next_z(s) - s
        fz, pz = cond_z[plane(i - 1), :] * dz, middle_z[plane(i - 1), :] * dz
        second[i, here] = (
            (decay[plane(i - 1), :] * s + heat[plane(i - 1), :])
            + (flux_next - flux)
            + (cond_y[i, here] * d_up - cond_y[i, below] * d_down)
            + (fz - last_z(fz))
        )
        mine[plane(i - 1), :] = (
            (prod_next + prod)
            + (middle_y[i, here] * d_up + middle_y[i, below] * d_down)
            + (pz + last_z(pz))
        )
        return s_next, flux_next, prod_next

    s = start[1, here]
    lax.fori_loop(1, cells_x + 1, second_plane, (s, cond_x[plane(0), :] * s, middle_x[plane(0), :] * s), unroll=UNROLL)

    def late_plane(i, carry):
        s, prod = carry
        s_next = second[i + 1, here]
        prod_next = late_x[plane(i), :] * (s_next - s)
        d_up, d_down = second[i, above] - s, s - second[i, below]
        pz = late_z[plane(i - 1), :] * (next_z(s) - s)
        mine[plane(i - 1), :] = (
            mine[plane(i - 1), :]
            + (prod_next + prod)
            + (late_y[i, here] * d_up + late_y[i, below] * d_down)
            + (pz + last_z(pz))
        )
        return s_next, prod_next

    def core_copy(index, source, target):
        return pltpu.make_async_remote_copy(
            src_ref=source,
            dst_ref=target,
            send_sem=core_send.at[index],
            recv_sem=core_recv.at[index],
            device_id=other_core,
            device_id_type=MESH,
        )

    chunk = cells_x // CHUNKS
    s = second[1, here]
    carry = (s, late_x[plane(0), :] * s)
    crossing = []
    for c in range(CHUNKS):
        carry = lax.fori_loop(1 + c * chunk, 1 + (c + 1) * chunk, late_plane, carry, unroll=UNROLL)
        part = pl.ds(c * chunk * cells_y, chunk * cells_y)
        crossing.append(core_copy(c, mine.at[part], theirs.at[part]))
        crossing[-1].start()

    wait_edges(START)
    wait_edges(SECOND)
    for c in range(4):
        @pl.when(beyond[c])
        def _():
            slot = halo_corner.at[corner_rows(c)]
            pltpu.make_async_copy(slot, slot, halo_recv.at[20 + c]).wait()

    known = [jnp.where(exists, f32(1), f32(0)) for exists in there]

    def added(add, add_next, add_last, inner_last, inner_next, up, down, z):
        pz = z * (next_z(add) - add)
        return (
            add * (inner_last - inner_next)
            + (up * (add_next - add) + down * (add - add_last))
            + (pz + last_z(pz))
        )

    for side, sign in ((0, -1.0), (1, 1.0)):
        i, face, inward = (1, 0, 1) if side == 0 else (cells_x, cells_x, cells_x - 1)
        near = x_slot(START, side)
        far = x_slot(SECOND, side)
        k = cond_x[plane(face), :]
        add = k * halo_x[near, :]
        halo_x[far, :] = halo_x[far, :] + known[side] * (k * start[i, here])
        for j in range(2):
            at = pl.ds((SECOND * 2 + side) * cells_y + j * (cells_y - 1), 1)
            halo_x[at, :] = halo_x[at, :] + halo_corner[pl.ds((side * 2 + j) * 8, 1), :]
        base = side * (cells_y + 2 * TOP) + TOP
        shift_x[pl.ds(base, cells_y), :] = add
        edge_mine[pl.ds(side * cells_y, cells_y), :] = added(
            add, shift_x[pl.ds(base + 1, cells_y), :], shift_x[pl.ds(base - 1, cells_y), :],
            late_x[plane(i - 1), :], late_x[plane(i), :],
            late_y[i, here], late_y[i, below], late_z[plane(i - 1), :],
        ) + sign * (
            middle_x[plane(face), :] * halo_x[near, :] + late_x[plane(face), :] * halo_x[far, :]
        )
        edge_mine[pl.ds((2 + side) * cells_y, cells_y), :] = sign * (add * late_x[plane(inward), :])

        y, face, inward = (0, -1, 0) if side == 0 else (cells_y - 1, cells_y - 1, cells_y - 2)
        near = y_slot(START, side)
        far = y_slot(SECOND, side)
        k = row(cond_y, face)
        add = k * halo_y[near, :]
        halo_y[far, :] = halo_y[far, :] + known[2 + side] * (k * row(start, y))
        for j in range(2):
            at = pl.ds((SECOND * 2 + side) * cells_x + j * (cells_x - 1), 1)
            halo_y[at, :] = halo_y[at, :] + halo_corner[pl.ds((j * 2 + side) * 8 + 1, 1), :]
        base = side * (cells_x + 2 * TOP) + TOP
        shift_y[pl.ds(base, cells_x), :] = add
        edges_y = 4 * cells_y + side * cells_x
        edge_mine[pl.ds(edges_y, cells_x), :] = added(
            add, shift_y[pl.ds(base + 1, cells_x), :], shift_y[pl.ds(base - 1, cells_x), :],
            row(late_y, y - 1), row(late_y, y),
            flat_row(late_x, y, 1), flat_row(late_x, y), flat_row(late_z, y),
        ) + sign * (row(middle_y, face) * halo_y[near, :] + row(late_y, face) * halo_y[far, :])
        edge_mine[pl.ds(edges_y + 2 * cells_x, cells_x), :] = sign * (add * row(late_y, inward))
    crossing.append(core_copy(CHUNKS, edge_mine, edge_theirs))
    crossing[-1].start()

    sent = outbox.at[pl.ds(0, (tiles - 1) * rows)]
    pltpu.make_async_copy(sent, sent, piece_send).wait()
    for field, ref in enumerate((cond, late, middle, start, second)):
        for side in range(4):
            @pl.when(there[side])
            def _():
                edge_copy(field, ref, side).wait_send()
    for c in range(4):
        @pl.when(beyond[c])
        def _():
            corner_copy(c).wait_send()
    for copy in crossing:
        copy.wait()


def finish_kernel(sizes, earliest, mine, theirs, edge_mine, edge_theirs, adjoint_out, gradient, total, copy_sem, part_sem):
    cells_x, cells_y = sizes
    chunk = cells_x // CHUNKS
    copies = []
    for c in range(CHUNKS):
        part = pl.ds(c * chunk * cells_y, chunk * cells_y)
        copies.append(pltpu.make_async_copy(earliest.at[part], adjoint_out.at[part], copy_sem.at[c]))
        copies[-1].start()
    for c in range(CHUNKS):
        part = pl.ds(c * chunk * cells_y, chunk * cells_y)
        total[part, :] = mine[part, :] + theirs[part, :]
        for depth in range(2):
            for side in range(2):
                if c == side * (CHUNKS - 1):
                    x = cells_x - 1 - depth if side else depth
                    here = pl.ds(x * cells_y, cells_y)
                    added = pl.ds((2 * depth + side) * cells_y, cells_y)
                    total[here, :] = total[here, :] + (edge_mine[added, :] + edge_theirs[added, :])
                y = cells_y - 1 - depth if side else depth
                here = pl.ds(c * chunk * cells_y + y, chunk, stride=cells_y)
                added = pl.ds(4 * cells_y + (2 * depth + side) * cells_x + c * chunk, chunk)
                total[here, :] = total[here, :] + (edge_mine[added, :] + edge_theirs[added, :])
        copies.append(pltpu.make_async_copy(total.at[part], gradient.at[part], part_sem.at[c]))
        copies[-1].start()
    for copy in copies:
        copy.wait()


def local(n_tx, n_ty, conductivity, cooling, source, adjoint_in, store, holder, step_index):
    cells_x, cells_y, cells_z = conductivity.shape
    _, held, _, tiles, piece = store.shape
    rows = piece // cells_z
    sizes = (n_tx, n_ty, cells_x, cells_y, cells_z, tiles, rows)
    flat = (cells_x * cells_y, cells_z)
    roomy = ((cells_x + 2) * cells_y, cells_z)
    padded = (cells_x + 3, 2 * TOP + cells_y, cells_z)
    edges = (4 * cells_y + 4 * cells_x, cells_z)
    f32 = jnp.float32

    def vmem(shape):
        return pltpu.VMEM(shape, f32)

    in_hbm = pl.BlockSpec(memory_space=pltpu.HBM)
    in_vmem = pl.BlockSpec(memory_space=pltpu.VMEM)
    shaped = jax.ShapeDtypeStruct
    results = pl.pallas_call(
        functools.partial(window_kernel, sizes),
        out_shape=[shaped(flat, f32)] * 3 + [shaped(edges, f32)] * 2,
        in_specs=[in_hbm] * 7,
        out_specs=[in_vmem] * 5,
        scratch_shapes=[
            pltpu.SMEM(step_index.shape, jnp.int32),
            pltpu.SMEM(holder.shape, jnp.int32),
            vmem((held, tiles, piece)),
            vmem(((tiles + 8) * rows, cells_z)),
            vmem((tiles, rows, cells_z)),
            *[vmem(flat)] * 2,
            *[vmem(roomy)] * 2,
            *[vmem(padded)] * 5,
            *[vmem(roomy), vmem(padded), vmem(roomy)] * 3,
            vmem((10 * cells_y, cells_z)),
            vmem((10 * cells_x, cells_z)),
            vmem((32, cells_z)),
            vmem((2 * cells_y, cells_z)),
            vmem((10 * cells_x, cells_z)),
            vmem((32, cells_z)),
            vmem((2 * (cells_y + 2 * TOP), cells_z)),
            vmem((2 * (cells_x + 2 * TOP), cells_z)),
            pltpu.SemaphoreType.DMA((7,)),
            *[pltpu.SemaphoreType.DMA] * 3,
            *[pltpu.SemaphoreType.DMA((24,))] * 2,
            *[pltpu.SemaphoreType.DMA((CHUNKS + 1,))] * 2,
        ],
        compiler_params=pltpu.CompilerParams(
            collective_id=0, has_side_effects=True, vmem_limit_bytes=50 << 20
        ),
    )(
        step_index,
        holder,
        conductivity.reshape(flat),
        cooling.reshape(flat),
        source.reshape(flat),
        adjoint_in.reshape(flat),
        store.reshape(held, tiles, piece),
    )
    adjoint_out, gradient = pl.pallas_call(
        functools.partial(finish_kernel, (cells_x, cells_y)),
        out_shape=[shaped(flat, f32)] * 2,
        in_specs=[in_vmem] * 5,
        out_specs=[in_hbm] * 2,
        scratch_shapes=[vmem(roomy), *[pltpu.SemaphoreType.DMA((CHUNKS,))] * 2],
        compiler_params=pltpu.CompilerParams(vmem_limit_bytes=4 << 20),
    )(*results)
    return adjoint_out.reshape(adjoint_in.shape), gradient.reshape(conductivity.shape)


def solution(mesh):
    in_specs = (
        P("tx", "ty", None),
        P("scen", "tx", "ty", None),
        P("scen", "tx", "ty", None),
        P("scen", "tx", "ty", None),
        P("scen", None, ("tx", "ty"), None, None),
        P(("tx", "ty"), None),
        P("scen"),
    )
    out_specs = (P("scen", "tx", "ty", None), P("tx", "ty", None))
    body = functools.partial(local, mesh.shape["tx"], mesh.shape["ty"])
    return jax.shard_map(body, mesh=mesh, in_specs=in_specs, out_specs=out_specs, check_vma=False)
```
